256 devices in a mesh: grp: 8 (over x, core), dev: 32 (over y, z).
Axes of the slice: x: 4, y: 4, z: 8, core: 2. Of those that a mesh axis runs over, the one named last changes fastest.
Arguments:
- tracer: float32 [96, 1048576], P(None, ('grp', 'dev')), may hold values from 0.05 to 2
- tile_rows: int32 [40960], P(('grp', 'dev')), may hold values from 0 to 8191, as said below
- tile_cols: int32 [40960], P(('grp', 'dev')), may hold values from 0 to 8191, as said below
- tile_values: bfloat16 [40960, 128, 128], P(('grp', 'dev')), may hold values from -0.25 to 0.25
- level_counts: int32 [32768], P(('grp', 'dev')), may hold values from 1 to 32, as said below
- column_owner: int32 [32768], P(('grp', 'dev')), may hold values from 0 to 31, as said below
- half_saturation: float32 [16], replicated, may hold values from 0.1 to 1
- growth_rate: float32 [64], replicated, may hold values from 0.2 to 2
- uptake: float32 [64, 16], replicated, may hold values from 0 to 0.125
- graze_preference: float32 [64, 64], replicated, may hold values from 0 to 0.03125
- graze_maximum: float32 [64], replicated, may hold values from 0.2 to 2
Outputs:
- updated: float32 [96, 1048576], P(None, ('grp', 'dev'))
- production: float32 [32768], P(('grp', 'dev'))
The draws below stay inside these ranges and needn't reach their ends.
Inputs may be any that keep to these rules, and one draw needn't show every extreme that they name: `tile_rows`: each device holds 160 tiles; taken device after device along dev, the tiles of a group run in increasing row block. Device d of the whole chain of devices owns row blocks d * 32 to d * 32 + 31; its tiles have row blocks of its own or, among its first 20 tiles only, of the device before it in its group. Device 1 of every group holds exactly 20 tiles of device 0's row blocks. `tile_cols`: A tile's column block lies within 16 blocks of its row block, and within the blocks owned by the device that holds the tile and its two neighbours in the chain. `level_counts`: every device's first column has 32 wet levels, its second one 1. `column_owner`: every device sends exactly 4 of its columns to each device of its group.
All inputs are finite; a program needn't handle non-finite values.
Results may differ from the reference program's by a relative error of at most 0.0018.
Values may be sent and summed in bfloat16 or wider, within the bound.
A program may use at most 64 MiB of HBM per device.

```python
import math
import jax
import jax.numpy as jnp
from jax import lax

NUT = 16
PLK = 64
NTR = 96
LEV = 32
COLS_DEV = 128
BLK = 128
TPB = 5
CD = 4096
BPD = 32
NT = 160
SPILL = 20
R = 16
NCELL = 1048576
TILES = 40960
N_GRP = 8
N_DEV = 32


def tile_pattern(key):
    device_count = N_GRP * N_DEV
    spill_key = jax.random.fold_in(key, 11)
    offset_key = jax.random.fold_in(key, 12)
    owner_ids = jnp.arange(N_DEV, dtype=jnp.int32)
    spill_count = jax.random.randint(spill_key, (N_GRP, N_DEV), 0, SPILL + 1)
    spill_count = jnp.where(owner_ids[None, :] == 0, SPILL, spill_count)
    spill_count = jnp.where(owner_ids[None, :] == N_DEV - 1, 0, spill_count)
    range_end = (owner_ids[None, :] + 1) * NT + spill_count
    range_start = jnp.concatenate([jnp.zeros((N_GRP, 1), jnp.int32), range_end[:, :-1]], axis=1)
    position = jnp.arange(N_DEV * NT, dtype=jnp.int32)
    owner_index = jnp.sum((range_end[:, None, :] <= position[None, :, None]).astype(jnp.int32), axis=2)
    first_tile = jnp.take_along_axis(range_start, owner_index, axis=1)
    tile_count = jnp.take_along_axis(range_end - range_start, owner_index, axis=1)
    offset_inside = position[None, :] - first_tile
    head_count = tile_count - SPILL
    head_blocks = BPD - SPILL
    in_head = offset_inside < head_count
    head_block = offset_inside * head_blocks // head_count
    head_rank = offset_inside - (head_block * head_count + head_blocks - 1) // head_blocks
    tail_index = offset_inside - head_count
    block_inside = jnp.where(in_head, head_block, head_blocks + tail_index)
    groups = jnp.arange(N_GRP, dtype=jnp.int32)[:, None]
    owner_first = groups * (N_DEV * BPD) + owner_index * BPD
    row_blocks = owner_first + block_inside
    offset_draw = jax.random.randint(offset_key, row_blocks.shape, -R, R + 1)
    head_offset = jnp.where(head_rank == 0, 0, jnp.where(head_rank == 1, -R, jnp.where(head_rank == 2, R, offset_draw)))
    tail_offset = jnp.where(tail_index % 2 == 0, -R, offset_draw)
    head_cols = jnp.clip(row_blocks + head_offset, 0, device_count * BPD - 1)
    tail_cols = jnp.clip(jnp.maximum(row_blocks + tail_offset, owner_first), 0, device_count * BPD - 1)
    col_blocks = jnp.where(in_head, head_cols, tail_cols)
    return (row_blocks.reshape(-1).astype(jnp.int32), col_blocks.reshape(-1).astype(jnp.int32))


def column_pattern(key):
    device_count = N_GRP * N_DEV
    level_key = jax.random.fold_in(key, 21)
    order_key = jax.random.fold_in(key, 22)
    shuffle_key = jax.random.fold_in(key, 23)
    levels = jax.random.randint(level_key, (device_count, COLS_DEV), 1, LEV + 1)
    column_ids = jnp.arange(COLS_DEV, dtype=jnp.int32)
    levels = jnp.where(column_ids[None, :] == 0, LEV, jnp.where(column_ids[None, :] == 1, 1, levels))
    tie_break = jnp.argsort(jax.random.randint(order_key, (device_count, COLS_DEV), 0, 2 ** 30), axis=1, stable=True)
    depth_score = levels * COLS_DEV + tie_break
    depth_rank = jnp.argsort(jnp.argsort(-depth_score, axis=1, stable=True), axis=1, stable=True)
    band_index = depth_rank // N_DEV
    place_index = depth_rank % N_DEV
    slot_index = jnp.where(band_index % 2 == 0, place_index, N_DEV - 1 - place_index)
    shuffle = jnp.argsort(jax.random.randint(shuffle_key, (device_count, N_DEV), 0, 2 ** 30), axis=1, stable=True)
    owner_index = jnp.take_along_axis(shuffle, slot_index, axis=1)
    return (levels.reshape(-1).astype(jnp.int32), owner_index.reshape(-1).astype(jnp.int32))


def draw_tile_rows(key, part):
    return tile_pattern(key)[0]


def draw_tile_cols(key, part):
    return tile_pattern(key)[1]


def draw_level_counts(key, part):
    return column_pattern(key)[0]


def draw_column_owner(key, part):
    return column_pattern(key)[1]


def block_scale(own_key, dims, cuts, least, high):
    gain = 1.0
    for dim, shards_of in cuts:
        draws = jax.random.uniform(jax.random.fold_in(jax.random.fold_in(own_key, 6), dim), (shards_of,), jnp.float32, least / len(cuts), high / len(cuts))
        gain = gain * jnp.repeat(jnp.exp(draws), dims[dim] // shards_of).reshape((-1,) + (1,) * (len(dims) - 1 - dim))
    return gain


def gaussian(own_key, extent, width, most, pieces=(), held_as=jnp.bfloat16):
    result = width * jax.random.normal(own_key, extent, jnp.float32)
    if pieces:
        result = result * block_scale(own_key, extent, pieces, -0.22, 0.18)
    return jnp.clip(result, -most, most).astype(held_as)


def setup_inputs(seed: int = 0) -> dict:
    key_of = jax.random.split(jax.random.key(seed), 12)
    return {
        "tracer": jnp.clip(0.05 + 1.95 * jax.random.uniform(key_of[0], (NTR, NCELL), jnp.float32) ** block_scale(key_of[0], (NTR, NCELL), ((1, 256),), -0.2, 0.2), 0.05, 2.0),
        "tile_rows": draw_tile_rows(jax.random.fold_in(key_of[11], 71), 0),
        "tile_cols": draw_tile_cols(jax.random.fold_in(key_of[11], 71), 0),
        "tile_values": gaussian(key_of[3], (TILES, BLK, BLK), (TPB * BLK) ** -0.5, 0.25, ((0, 256),)),
        "level_counts": draw_level_counts(jax.random.fold_in(key_of[11], 71), 0),
        "column_owner": draw_column_owner(jax.random.fold_in(key_of[11], 71), 0),
        "half_saturation": jnp.clip(jnp.exp(jax.random.uniform(key_of[6], (NUT,), jnp.float32, math.log(0.1), math.log(1.0))), 0.1, 1.0),
        "growth_rate": jnp.clip(jnp.exp(jax.random.uniform(key_of[7], (PLK,), jnp.float32, math.log(0.2), math.log(2.0))), 0.2, 2.0),
        "uptake": jnp.clip(jax.random.uniform(key_of[8], (PLK, NUT), jnp.float32, 0.0, 0.125), 0.0, 0.125),
        "graze_preference": jnp.clip(jax.random.uniform(key_of[9], (PLK, PLK), jnp.float32, 0.0, 0.03125), 0.0, 0.03125),
        "graze_maximum": jnp.clip(jnp.exp(jax.random.uniform(key_of[10], (PLK,), jnp.float32, math.log(0.2), math.log(2.0))), 0.2, 2.0),
    }


highest = lax.Precision.HIGHEST
WATER_DECAY = 0.03
SHADE_DECAY = 0.05
EFFICIENCY = 0.3
MORTALITY = 0.1
REMINERAL = 0.2
TIMESTEP = 0.5


def ecosystem(cells, levels, half_saturation, growth_rate, uptake, graze_preference, graze_maximum):
    column_count = levels.shape[0]
    depth_index = lax.broadcasted_iota(jnp.int32, (column_count, LEV), 1).astype(jnp.float32)
    wet_mask = (depth_index < levels[:, None]).astype(jnp.float32).reshape(1, column_count * LEV)
    nutrient = cells[:NUT]
    plankton = cells[NUT:NUT + PLK]
    detritus = cells[NUT + PLK:]
    chlorophyll = (jnp.sum(plankton, axis=0, keepdims=True) / PLK * wet_mask).reshape(column_count, LEV)
    above_mask = (lax.broadcasted_iota(jnp.int32, (LEV, LEV), 0) < lax.broadcasted_iota(jnp.int32, (LEV, LEV), 1)).astype(jnp.float32)
    shading = jnp.dot(chlorophyll, above_mask, precision=highest).reshape(1, column_count * LEV)
    sunlight = jnp.exp(-WATER_DECAY * depth_index.reshape(1, column_count * LEV) - SHADE_DECAY * shading)
    monod_term = nutrient / (nutrient + half_saturation[:, None])
    limitation = jnp.dot(uptake, monod_term, precision=highest)
    capacity = growth_rate[:, None] * sunlight * plankton
    growth = capacity * limitation
    food_sum = jnp.dot(graze_preference, plankton, precision=highest)
    graze_rate = graze_maximum[:, None] * plankton / (1.0 + food_sum)
    grazed = plankton * jnp.dot(graze_preference.T, graze_rate, precision=highest)
    eaten_total = graze_rate * food_sum
    d_plankton = growth - grazed + EFFICIENCY * eaten_total - MORTALITY * plankton
    d_nutrient = -monod_term * jnp.dot(uptake.T, capacity, precision=highest) + REMINERAL * detritus
    waste_flux = ((1.0 - EFFICIENCY) * eaten_total + MORTALITY * plankton).reshape(NUT, PLK // NUT, column_count * LEV)
    d_detritus = jnp.sum(waste_flux, axis=1) - REMINERAL * detritus
    source = jnp.concatenate([d_nutrient, d_plankton, d_detritus], axis=0) * wet_mask
    column_sum = jnp.sum((jnp.sum(growth, axis=0) / PLK * wet_mask[0]).reshape(column_count, LEV), axis=1)
    return source, column_sum


def reference(tracer, tile_rows, tile_cols, tile_values, level_counts, column_owner, half_saturation, growth_rate, uptake, graze_preference, graze_maximum):
    device_count = N_GRP * N_DEV
    block_count = device_count * BPD
    coarse = lax.optimization_barrier(tracer.astype(jnp.bfloat16))
    blocks = coarse.astype(jnp.float32).reshape(NTR, block_count, BLK).transpose(1, 0, 2)
    row_blocks = tile_rows.reshape(device_count, NT)
    col_blocks = tile_cols.reshape(device_count, NT)
    tile_data = tile_values.reshape(device_count, NT, BLK, BLK)

    def add_device(running, tile_batch):
        batch_rows, batch_cols, batch_data = tile_batch
        picked = blocks[batch_cols]
        contrib = jnp.einsum("tcb,tab->tca", picked, batch_data.astype(jnp.float32), precision=highest)
        return running.at[batch_rows].add(contrib), None

    running, _ = lax.scan(add_device, jnp.zeros((block_count, NTR, BLK), jnp.float32), (row_blocks, col_blocks, tile_data))
    transport = running.transpose(1, 0, 2).reshape(NTR, block_count * BLK)

    shards = tracer.reshape(NTR, device_count, CD).transpose(1, 0, 2)
    shard_levels = level_counts.reshape(device_count, COLS_DEV).astype(jnp.float32)

    def one_device(pair):
        return ecosystem(pair[0], pair[1], half_saturation, growth_rate, uptake, graze_preference, graze_maximum)

    sources, column_sums = lax.map(one_device, (shards, shard_levels))
    source = sources.transpose(1, 0, 2).reshape(NTR, device_count * CD)
    updated = tracer + transport + TIMESTEP * source

    owners = column_owner.reshape(N_GRP, N_DEV, COLS_DEV)
    send_order = jnp.argsort(owners, axis=2, stable=True).astype(jnp.int32)
    sorted_sums = jnp.take_along_axis(column_sums.reshape(N_GRP, N_DEV, COLS_DEV), send_order, axis=2)
    production = sorted_sums.reshape(N_GRP, N_DEV, N_DEV, COLS_DEV // N_DEV).transpose(0, 2, 1, 3).reshape(N_GRP * N_DEV * COLS_DEV)
    return updated, production
```

```python
import functools

import jax
import jax.numpy as jnp
from jax import lax
from jax.experimental import pallas as pl
from jax.experimental.pallas import tpu as pltpu
from jax.sharding import PartitionSpec as P

MESH = pl.DeviceIdType.MESH
F32 = jnp.float32
BF16 = jnp.bfloat16

NUT = 16
PLK = 64
NTR = 96
LEV = 32
COLS = 128
BLK = 128
BPD = 32
NT = 160
SPILL = 20
REACH = 16
CD = BPD * BLK
NZ = 8
WATER_DECAY = 0.03
SHADE_DECAY = 0.05
EFFICIENCY = 0.3
MORTALITY = 0.1
REMINERAL = 0.2
TIMESTEP = 0.5

TILE_CHUNKS = 5
TILES_SENT = SPILL // TILE_CHUNKS
GROUP = 256
UNROLL = 8
SMALL = 7


def iota(shape, dim):
    return lax.broadcasted_iota(jnp.int32, shape, dim)


def split2(x):
    high = x.astype(BF16)
    return high, (x - high.astype(F32)).astype(BF16)


def split3(x):
    high = x.astype(BF16)
    rest = x - high.astype(F32)
    middle = rest.astype(BF16)
    return high, middle, (rest - middle.astype(F32)).astype(BF16)


def weights3(w):
    high, low = split2(w)
    return jnp.concatenate([high, high, low], axis=1)


def data3(x):
    high, low = split2(x)
    return jnp.concatenate([high, low, high], axis=0)


def matmul(a, b):
    return jnp.dot(a, b, preferred_element_type=F32)


def matmul_nt(a, b):
    return lax.dot_general(a, b, (((1,), (1,)), ((), ())), preferred_element_type=F32)


def column_of(row):
    n = row.shape[1]
    return jnp.sum(jnp.where(iota((n, n), 0) == iota((n, n), 1), row, 0.0), axis=1, keepdims=True)


def kernel(
    n_grp,
    n_dev,
    tracer,
    tile_rows,
    tile_cols,
    tiles,
    levels,
    owner,
    half_saturation,
    growth_rate,
    uptake,
    preference,
    graze_maximum,
    updated,
    production,
    tr,
    ext,
    own_tiles,
    got_tiles,
    runs,
    got_runs,
    levels_v,
    owner_v,
    half_v,
    growth_v,
    uptake_v,
    preference_v,
    maximum_v,
    chl,
    wet,
    sun,
    grown,
    w_limit,
    w_food,
    w_graze,
    w_use,
    to_z,
    from_z,
    to_y,
    from_y,
    got_rows,
    got_cols,
    place,
    got_place,
    tracer_sem,
    tiles_sem,
    small_sem,
    halo_send,
    halo_recv,
    spill_send,
    spill_recv,
    rows_sem,
    z_send,
    z_recv,
    y_send,
    y_recv,
):
    ny = n_dev // NZ
    grp = lax.axis_index("grp")
    dev = lax.axis_index("dev")
    me_y = dev // NZ
    me_z = lax.rem(dev, NZ)
    position = grp * n_dev + dev
    count = n_grp * n_dev
    after = lax.rem(position + 1, count)
    before = lax.rem(position + count - 1, count)
    right = (after // n_dev, lax.rem(after, n_dev))
    left = (before // n_dev, lax.rem(before, n_dev))
    z_peers = [(grp, me_y * NZ + lax.rem(me_z + k, NZ)) for k in range(1, NZ)]
    y_peers = [(grp, lax.rem(me_y + k, ny) * NZ + me_z) for k in range(1, ny)]

    barrier = pltpu.get_barrier_semaphore()
    for peer in [left, right] + z_peers + y_peers:
        pl.semaphore_signal(barrier, inc=1, device_id=peer, device_id_type=MESH)

    load = pltpu.make_async_copy(tracer, tr, tracer_sem)
    load.start()
    small = [
        pltpu.make_async_copy(source, target, small_sem.at[i])
        for i, (source, target) in enumerate(
            [
                (levels, levels_v),
                (owner, owner_v),
                (half_saturation, half_v),
                (growth_rate, growth_v),
                (uptake, uptake_v),
                (preference, preference_v),
                (graze_maximum, maximum_v),
            ]
        )
    ]
    for copy in small:
        copy.start()
    load_tiles = pltpu.make_async_copy(tiles, own_tiles, tiles_sem)
    load_tiles.start()

    load.wait()
    for b in range(BPD):
        ext[REACH + b] = tr[:, b * BLK : (b + 1) * BLK].astype(BF16)

    pl.semaphore_wait(barrier, 2 + (NZ - 1) + (ny - 1))

    def remote(source, target, send, recv, peer):
        return pltpu.make_async_remote_copy(
            src_ref=source,
            dst_ref=target,
            send_sem=send,
            recv_sem=recv,
            device_id=peer,
            device_id_type=MESH,
        )

    index_copies = [
        remote(tile_rows, got_rows, rows_sem.at[0], rows_sem.at[1], left),
        remote(tile_cols, got_cols, rows_sem.at[2], rows_sem.at[3], left),
    ]
    halo = [
        remote(
            ext.at[pl.ds(REACH, REACH)],
            ext.at[pl.ds(REACH + BPD, REACH)],
            halo_send.at[0],
            halo_recv.at[0],
            left,
        ),
        remote(
            ext.at[pl.ds(BPD, REACH)],
            ext.at[pl.ds(0, REACH)],
            halo_send.at[1],
            halo_recv.at[1],
            right,
        ),
    ]
    spill = [
        remote(
            tiles.at[pl.ds(c * TILES_SENT, TILES_SENT)],
            got_tiles.at[pl.ds(c * TILES_SENT, TILES_SENT)],
            spill_send.at[c],
            spill_recv.at[c],
            left,
        )
        for c in range(TILE_CHUNKS)
    ]
    for copy in halo:
        copy.start()
    for copy in index_copies:
        copy.start()
    for copy in spill:
        copy.start()

    for copy in small:
        copy.wait()
    w_limit[...] = weights3(uptake_v[...])
    w_food[...] = weights3(preference_v[...])
    w_graze[...] = weights3(preference_v[...].T)
    w_use[...] = weights3(uptake_v[...].T)
    half = column_of(half_v[...])
    growth_column = column_of(growth_v[...])
    maximum = column_of(maximum_v[...])

    column_row = iota((BPD, COLS), 1)
    pick_row = (column_row >> 2) == iota((BPD, COLS), 0)
    in_block = ((iota((COLS, BLK), 0) & 3) == (iota((COLS, BLK), 1) >> 5)).astype(BF16)
    level_row = jnp.where(pick_row, levels_v[...].astype(F32), 0.0).astype(BF16)
    wet_levels = matmul(level_row, in_block)
    depth = (iota((BPD, BLK), 1) & (LEV - 1)).astype(F32)
    wet_mask = (depth < wet_levels).astype(F32)
    wet[...] = wet_mask

    def sum_plankton(i, carry):
        lanes = pl.ds(pl.multiple_of(i * BLK, BLK), BLK)
        chl[pl.ds(i, 1), :] = jnp.sum(tr[NUT : NUT + PLK, lanes], axis=0, keepdims=True)
        return carry

    lax.fori_loop(0, BPD, sum_plankton, 0, unroll=4)
    upper_row, upper_col = iota((2 * BLK, BLK), 0) & (BLK - 1), iota((2 * BLK, BLK), 1)
    above = ((upper_row < upper_col) & ((upper_row >> 5) == (upper_col >> 5))).astype(BF16)
    chl_high, chl_low = split2(chl[...] * (1.0 / PLK) * wet_mask)
    shading = matmul(jnp.concatenate([chl_high, chl_low], axis=1), above)
    sun[...] = jnp.exp(-WATER_DECAY * depth - SHADE_DECAY * shading)

    fold_col = iota((NUT, 2 * PLK), 1) & (PLK - 1)
    fold = ((fold_col >> 2) == iota((NUT, 2 * PLK), 0)).astype(BF16)
    per_group = GROUP // BLK

    def row_of(ref, i):
        return jnp.concatenate([ref[pl.ds(i * per_group + h, 1), :] for h in range(per_group)], axis=1)

    def ecosystem(i, carry):
        lanes = pl.ds(pl.multiple_of(i * GROUP, GROUP), GROUP)
        mask = row_of(wet, i) * TIMESTEP
        light = row_of(sun, i)
        nutrient = tr[:NUT, lanes]
        plankton = tr[NUT : NUT + PLK, lanes]
        detritus = tr[NUT + PLK :, lanes]
        monod = nutrient / (nutrient + half)
        limitation = matmul(w_limit[...], data3(monod))
        capacity = growth_column * (light * plankton)
        growth = capacity * limitation
        food = matmul(w_food[...], data3(plankton))
        rate = maximum * plankton / (1.0 + food)
        eaten = rate * food
        grazed = plankton * matmul(w_graze[...], data3(rate))
        mortality = MORTALITY * plankton
        d_plankton = growth - grazed + EFFICIENCY * eaten - mortality
        use = matmul(w_use[...], data3(capacity))
        d_nutrient = REMINERAL * detritus - monod * use
        waste = (1.0 - EFFICIENCY) * eaten + mortality
        d_detritus = matmul(fold, jnp.concatenate(split2(waste), axis=0)) - REMINERAL * detritus
        updated[:NUT, lanes] = nutrient + mask * d_nutrient
        updated[NUT : NUT + PLK, lanes] = plankton + mask * d_plankton
        updated[NUT + PLK :, lanes] = detritus + mask * d_detritus
        total = jnp.sum(growth, axis=0, keepdims=True)
        for h in range(per_group):
            grown[pl.ds(i * per_group + h, 1), :] = total[:, h * BLK : (h + 1) * BLK]
        return carry

    lax.fori_loop(0, CD // GROUP, ecosystem, 0)

    summed = jnp.concatenate(split3(grown[...] * (1.0 / PLK) * wet_mask), axis=1)
    lane_row, lane_col = iota((3 * BLK, COLS), 0) & (BLK - 1), iota((3 * BLK, COLS), 1)
    gather_columns = ((lane_row >> 5) == (lane_col & 3)).astype(BF16)
    by_block = matmul(summed, gather_columns)
    column_sum = jnp.sum(jnp.where(pick_row, by_block, 0.0), axis=0, keepdims=True)
    slot = iota((8 * NZ, COLS), 0)
    slot_owner = (slot & 7) * NZ + (slot >> 3)
    mine = (slot_owner == owner_v[...]) & ((slot & 7) < ny)
    mine_f = mine.astype(F32)
    earlier = (iota((COLS, COLS), 0) < iota((COLS, COLS), 1)).astype(BF16)
    seen = matmul(mine_f.astype(BF16), earlier)
    rank = jnp.sum(mine_f * seen, axis=0, keepdims=True)
    target = rank + (dev * (COLS // n_dev)).astype(F32)
    put = (iota((COLS, COLS), 0).astype(F32) == target).astype(BF16)
    sums = jnp.concatenate(split3(jnp.where(mine, column_sum, 0.0)), axis=1)
    to_z[...] = matmul_nt(sums, jnp.concatenate([put, put, put], axis=1)).reshape(NZ, 8, COLS)
    from_z[me_z] = to_z[me_z]
    z_copies = [
        remote(to_z.at[lax.rem(me_z + k, NZ)], from_z.at[me_z], z_send.at[k], z_recv.at[k], z_peers[k - 1])
        for k in range(1, NZ)
    ]
    for copy in z_copies:
        copy.start()

    first_row = position * BPD

    def find(rows, limit, length, steps, wanted):
        found = jnp.int32(0)
        for step in steps:
            trial = found + step
            at = rows[jnp.minimum(trial, length) - 1]
            found = jnp.where((trial <= length) & (at <= wanted), trial, found)
        last = jnp.maximum(found - 1, 0)
        return last, jnp.where((found > 0) & (rows[last] == wanted), 1, 0)

    def find_own(r, carry):
        last, held = find(tile_rows, NT, NT, (128, 64, 32, 16, 8, 4, 2, 1), first_row + r)
        place[0, r] = last
        place[1, r] = held
        return carry

    lax.fori_loop(0, BPD, find_own, 0)
    for copy in index_copies:
        copy.wait()

    def find_got(r, carry):
        last, held = find(got_rows, SPILL, SPILL, (16, 8, 4, 2, 1), first_row + r)
        got_place[0, r] = last
        got_place[1, r] = held
        return carry

    lax.fori_loop(0, BPD, find_got, 0)

    load_tiles.wait()
    for copy in halo:
        copy.wait()

    first_col = first_row - REACH

    def own(t, run):
        block = jnp.clip(tile_cols[t] - first_col, 0, BPD + 2 * REACH - 1)
        term = matmul_nt(ext[block], own_tiles[t])
        goes_on = tile_rows[t] == tile_rows[jnp.maximum(t - 1, 0)]
        run = jnp.where(goes_on, run, 0.0) + term
        runs[t] = run
        return run

    lax.fori_loop(0, NT, own, jnp.zeros((NTR, BLK), F32), unroll=UNROLL)

    for r in range(BPD):
        lanes = slice(r * BLK, (r + 1) * BLK)
        updated[:, lanes] += jnp.where(place[1, r] == 1, runs[place[0, r]], 0.0)

    for copy in z_copies:
        copy.wait()
    over_z = from_z[0]
    for k in range(1, NZ):
        over_z += from_z[k]
    to_y[...] = over_z
    from_y[me_y] = over_z
    y_copies = [
        remote(to_y, from_y.at[me_y], y_send.at[k], y_recv.at[k], y_peers[k - 1]) for k in range(1, ny)
    ]
    for copy in y_copies:
        copy.start()

    run = jnp.zeros((NTR, BLK), F32)
    for c in range(TILE_CHUNKS):
        spill[c].wait()
        for s in range(c * TILES_SENT, (c + 1) * TILES_SENT):
            block = jnp.clip(got_cols[s] - first_col, 0, BPD + 2 * REACH - 1)
            term = matmul_nt(ext[block], got_tiles[s])
            goes_on = got_rows[s] == got_rows[max(s - 1, 0)]
            run = jnp.where(goes_on, run, 0.0) + term
            got_runs[s] = run

    for r in range(BPD):
        lanes = slice(r * BLK, (r + 1) * BLK)
        updated[:, lanes] += jnp.where(got_place[1, r] == 1, got_runs[got_place[0, r]], 0.0)

    for copy in y_copies:
        copy.wait()
    over_y = from_y[0]
    for k in range(1, ny):
        over_y += from_y[k]
    in_row = iota((8, COLS), 0) == me_y
    production[...] = jnp.sum(jnp.where(in_row, over_y, 0.0), axis=0, keepdims=True)


def per_device(
    n_grp,
    n_dev,
    tracer,
    tile_rows,
    tile_cols,
    tile_values,
    level_counts,
    column_owner,
    half_saturation,
    growth_rate,
    uptake,
    graze_preference,
    graze_maximum,
):
    ny = n_dev // NZ
    anywhere = pl.BlockSpec(memory_space=pl.ANY)
    scalars = pl.BlockSpec(memory_space=pltpu.SMEM)
    vector = pl.BlockSpec(memory_space=pltpu.VMEM)
    dma = pltpu.SemaphoreType.DMA
    updated, production = pl.pallas_call(
        functools.partial(kernel, n_grp, n_dev),
        out_shape=(
            jax.ShapeDtypeStruct((NTR, CD), F32),
            jax.ShapeDtypeStruct((1, COLS), F32),
        ),
        in_specs=[anywhere, scalars, scalars] + [anywhere] * 8,
        out_specs=(vector, vector),
        scratch_shapes=[
            pltpu.VMEM((NTR, CD), F32),
            pltpu.VMEM((BPD + 2 * REACH, NTR, BLK), BF16),
            pltpu.VMEM((NT, BLK, BLK), BF16),
            pltpu.VMEM((SPILL, BLK, BLK), BF16),
            pltpu.VMEM((NT, NTR, BLK), F32),
            pltpu.VMEM((SPILL, NTR, BLK), F32),
            pltpu.VMEM((1, COLS), jnp.int32),
            pltpu.VMEM((1, COLS), jnp.int32),
            pltpu.VMEM((1, NUT), F32),
            pltpu.VMEM((1, PLK), F32),
            pltpu.VMEM((PLK, NUT), F32),
            pltpu.VMEM((PLK, PLK), F32),
            pltpu.VMEM((1, PLK), F32),
            pltpu.VMEM((BPD, BLK), F32),
            pltpu.VMEM((BPD, BLK), F32),
            pltpu.VMEM((BPD, BLK), F32),
            pltpu.VMEM((BPD, BLK), F32),
            pltpu.VMEM((PLK, 3 * NUT), BF16),
            pltpu.VMEM((PLK, 3 * PLK), BF16),
            pltpu.VMEM((PLK, 3 * PLK), BF16),
            pltpu.VMEM((NUT, 3 * PLK), BF16),
            pltpu.VMEM((NZ, 8, COLS), F32),
            pltpu.VMEM((NZ, 8, COLS), F32),
            pltpu.VMEM((8, COLS), F32),
            pltpu.VMEM((ny, 8, COLS), F32),
            pltpu.SMEM((NT,), jnp.int32),
            pltpu.SMEM((NT,), jnp.int32),
            pltpu.SMEM((2, BPD), jnp.int32),
            pltpu.SMEM((2, BPD), jnp.int32),
            dma,
            dma,
            dma((SMALL,)),
            dma((2,)),
            dma((2,)),
            dma((TILE_CHUNKS,)),
            dma((TILE_CHUNKS,)),
            dma((4,)),
            dma((NZ,)),
            dma((NZ,)),
            dma((ny,)),
            dma((ny,)),
        ],
        compiler_params=pltpu.CompilerParams(
            collective_id=0, has_side_effects=True, vmem_limit_bytes=56 * 1024 * 1024
        ),
        name="plankton_step",
    )(
        tracer,
        tile_rows,
        tile_cols,
        tile_values,
        level_counts.reshape(1, COLS),
        column_owner.reshape(1, COLS),
        half_saturation.reshape(1, NUT),
        growth_rate.reshape(1, PLK),
        uptake,
        graze_preference,
        graze_maximum.reshape(1, PLK),
    )
    return updated, production.reshape(COLS)


def solution(mesh):
    n_grp, n_dev = mesh.shape["grp"], mesh.shape["dev"]
    chain = P(("grp", "dev"))
    cells = P(None, ("grp", "dev"))
    return jax.shard_map(
        functools.partial(per_device, n_grp, n_dev),
        mesh=mesh,
        in_specs=(cells, chain, chain, P(("grp", "dev"), None, None), chain, chain, P(), P(), P(), P(), P()),
        out_specs=(cells, chain),
        check_vma=False,
    )
```

```python
import functools

import jax
import jax.numpy as jnp
from jax import lax
from jax.experimental import pallas as pl
from jax.experimental.pallas import tpu as pltpu
from jax.sharding import PartitionSpec as P

MESH = pl.DeviceIdType.MESH
F32 = jnp.float32
BF16 = jnp.bfloat16

NUT = 16
PLK = 64
NTR = 96
LEV = 32
COLS = 128
BLK = 128
BPD = 32
NT = 160
SPILL = 20
REACH = 16
CD = BPD * BLK
NZ = 8
WATER_DECAY = 0.03
SHADE_DECAY = 0.05
EFFICIENCY = 0.3
MORTALITY = 0.1
REMINERAL = 0.2
TIMESTEP = 0.5

TILE_CHUNKS = 5
TILES_SENT = SPILL // TILE_CHUNKS
GROUP = 256
UNROLL = 8
SMALL = 7


def iota(shape, dim):
    return lax.broadcasted_iota(jnp.int32, shape, dim)


def split2(x):
    high = x.astype(BF16)
    return high, (x - high.astype(F32)).astype(BF16)


def split3(x):
    high = x.astype(BF16)
    rest = x - high.astype(F32)
    middle = rest.astype(BF16)
    return high, middle, (rest - middle.astype(F32)).astype(BF16)


def weights3(w):
    high, low = split2(w)
    return jnp.concatenate([high, high, low], axis=1)


def data3(x):
    high, low = split2(x)
    return jnp.concatenate([high, low, high], axis=0)


def matmul(a, b):
    return jnp.dot(a, b, preferred_element_type=F32)


def matmul_nt(a, b):
    return lax.dot_general(a, b, (((1,), (1,)), ((), ())), preferred_element_type=F32)


def column_of(row):
    n = row.shape[1]
    return jnp.sum(jnp.where(iota((n, n), 0) == iota((n, n), 1), row, 0.0), axis=1, keepdims=True)


def kernel(
    n_grp,
    n_dev,
    tracer,
    tile_rows,
    tile_cols,
    tiles,
    levels,
    owner,
    half_saturation,
    growth_rate,
    uptake,
    preference,
    graze_maximum,
    updated,
    production,
    tr,
    ext,
    own_tiles,
    got_tiles,
    runs,
    got_runs,
    levels_v,
    owner_v,
    half_v,
    growth_v,
    uptake_v,
    preference_v,
    maximum_v,
    chl,
    wet,
    sun,
    grown,
    w_limit,
    w_food,
    w_graze,
    w_use,
    to_z,
    from_z,
    to_y,
    from_y,
    got_rows,
    got_cols,
    place,
    got_place,
    tracer_sem,
    tiles_sem,
    small_sem,
    halo_send,
    halo_recv,
    spill_send,
    spill_recv,
    rows_sem,
    z_send,
    z_recv,
    y_send,
    y_recv,
):
    ny = n_dev // NZ
    grp = lax.axis_index("grp")
    dev = lax.axis_index("dev")
    me_y = dev // NZ
    me_z = lax.rem(dev, NZ)
    position = grp * n_dev + dev
    count = n_grp * n_dev
    after = lax.rem(position + 1, count)
    before = lax.rem(position + count - 1, count)
    right = (after // n_dev, lax.rem(after, n_dev))
    left = (before // n_dev, lax.rem(before, n_dev))
    z_peers = [(grp, me_y * NZ + lax.rem(me_z + k, NZ)) for k in range(1, NZ)]
    y_peers = [(grp, lax.rem(me_y + k, ny) * NZ + me_z) for k in range(1, ny)]

    barrier = pltpu.get_barrier_semaphore()
    for peer in [left, right] + z_peers + y_peers:
        pl.semaphore_signal(barrier, inc=1, device_id=peer, device_id_type=MESH)

    load = pltpu.make_async_copy(tracer, tr, tracer_sem)
    load.start()
    small = [
        pltpu.make_async_copy(source, target, small_sem.at[i])
        for i, (source, target) in enumerate(
            [
                (levels, levels_v),
                (owner, owner_v),
                (half_saturation, half_v),
                (growth_rate, growth_v),
                (uptake, uptake_v),
                (preference, preference_v),
                (graze_maximum, maximum_v),
            ]
        )
    ]
    for copy in small:
        copy.start()
    load_tiles = pltpu.make_async_copy(tiles, own_tiles, tiles_sem)
    load_tiles.start()

    pl.semaphore_wait(barrier, 2 + (NZ - 1) + (ny - 1))

    def remote(source, target, send, recv, peer):
        return pltpu.make_async_remote_copy(
            src_ref=source,
            dst_ref=target,
            send_sem=send,
            recv_sem=recv,
            device_id=peer,
            device_id_type=MESH,
        )

    index_copies = [
        remote(tile_rows, got_rows, rows_sem.at[0], rows_sem.at[1], left),
        remote(tile_cols, got_cols, rows_sem.at[2], rows_sem.at[3], left),
    ]
    halo = [
        remote(
            ext.at[pl.ds(REACH, REACH)],
            ext.at[pl.ds(REACH + BPD, REACH)],
            halo_send.at[0],
            halo_recv.at[0],
            left,
        ),
        remote(
            ext.at[pl.ds(BPD, REACH)],
            ext.at[pl.ds(0, REACH)],
            halo_send.at[1],
            halo_recv.at[1],
            right,
        ),
    ]
    spill = [
        remote(
            (own_tiles if c else tiles).at[pl.ds(c * TILES_SENT, TILES_SENT)],
            got_tiles.at[pl.ds(c * TILES_SENT, TILES_SENT)],
            spill_send.at[c],
            spill_recv.at[c],
            left,
        )
        for c in range(TILE_CHUNKS)
    ]
    def round_blocks(first, blocks):
        for b in range(first, first + blocks):
            ext[REACH + b] = tr[:, b * BLK : (b + 1) * BLK].astype(BF16)

    spill[0].start()
    for copy in index_copies:
        copy.start()
    load.wait()
    round_blocks(0, REACH)
    halo[0].start()
    round_blocks(REACH, BPD - REACH)
    halo[1].start()

    for copy in small:
        copy.wait()
    w_limit[...] = weights3(uptake_v[...].T)
    w_food[...] = weights3(preference_v[...])
    w_graze[...] = weights3(preference_v[...].T)
    w_use[...] = weights3(uptake_v[...])
    half = column_of(half_v[...])
    growth_column = column_of(growth_v[...])
    maximum = column_of(maximum_v[...])

    column_row = iota((BPD, COLS), 1)
    pick_row = (column_row >> 2) == iota((BPD, COLS), 0)
    in_block = ((iota((COLS, BLK), 0) & 3) == (iota((COLS, BLK), 1) >> 5)).astype(BF16)
    level_row = jnp.where(pick_row, levels_v[...].astype(F32), 0.0).astype(BF16)
    wet_levels = matmul(level_row, in_block)
    depth = (iota((BPD, BLK), 1) & (LEV - 1)).astype(F32)
    wet_mask = (depth < wet_levels).astype(F32)
    wet[...] = wet_mask

    def sum_plankton(i, carry):
        lanes = pl.ds(pl.multiple_of(i * BLK, BLK), BLK)
        chl[pl.ds(i, 1), :] = jnp.sum(tr[NUT : NUT + PLK, lanes], axis=0, keepdims=True)
        return carry

    lax.fori_loop(0, BPD, sum_plankton, 0, unroll=4)
    upper_row, upper_col = iota((2 * BLK, BLK), 0) & (BLK - 1), iota((2 * BLK, BLK), 1)
    above = ((upper_row < upper_col) & ((upper_row >> 5) == (upper_col >> 5))).astype(BF16)
    chl_high, chl_low = split2(chl[...] * (1.0 / PLK) * wet_mask)
    shading = matmul(jnp.concatenate([chl_high, chl_low], axis=1), above)
    sun[...] = jnp.exp(-WATER_DECAY * depth - SHADE_DECAY * shading)

    fold_col = iota((NUT, 2 * PLK), 1) & (PLK - 1)
    fold = ((fold_col >> 2) == iota((NUT, 2 * PLK), 0)).astype(BF16)
    per_group = GROUP // BLK

    def row_of(ref, i):
        return jnp.concatenate([ref[pl.ds(i * per_group + h, 1), :] for h in range(per_group)], axis=1)

    def ecosystem(i, carry):
        lanes = pl.ds(pl.multiple_of(i * GROUP, GROUP), GROUP)
        mask = row_of(wet, i) * TIMESTEP
        light = row_of(sun, i)
        nutrient = tr[:NUT, lanes]
        plankton = tr[NUT : NUT + PLK, lanes]
        detritus = tr[NUT + PLK :, lanes]
        monod = nutrient / (nutrient + half)
        limitation = matmul(w_limit[...], data3(monod))
        capacity = growth_column * (light * plankton)
        growth = capacity * limitation
        food = matmul(w_food[...], data3(plankton))
        rate = maximum * plankton / (1.0 + food)
        eaten = rate * food
        grazed = plankton * matmul(w_graze[...], data3(rate))
        mortality = MORTALITY * plankton
        d_plankton = growth - grazed + EFFICIENCY * eaten - mortality
        use = matmul(w_use[...], data3(capacity))
        d_nutrient = REMINERAL * detritus - monod * use
        waste = (1.0 - EFFICIENCY) * eaten + mortality
        d_detritus = matmul(fold, jnp.concatenate(split2(waste), axis=0)) - REMINERAL * detritus
        updated[:NUT, lanes] = nutrient + mask * d_nutrient
        updated[NUT : NUT + PLK, lanes] = plankton + mask * d_plankton
        updated[NUT + PLK :, lanes] = detritus + mask * d_detritus
        total = jnp.sum(growth, axis=0, keepdims=True)
        for h in range(per_group):
            grown[pl.ds(i * per_group + h, 1), :] = total[:, h * BLK : (h + 1) * BLK]
        return carry

    lax.fori_loop(0, CD // GROUP, ecosystem, 0)

    summed = jnp.concatenate(split3(grown[...] * (1.0 / PLK) * wet_mask), axis=1)
    lane_row, lane_col = iota((3 * BLK, COLS), 0) & (BLK - 1), iota((3 * BLK, COLS), 1)
    gather_columns = ((lane_row >> 5) == (lane_col & 3)).astype(BF16)
    by_block = matmul(summed, gather_columns)
    column_sum = jnp.sum(jnp.where(pick_row, by_block, 0.0), axis=0, keepdims=True)
    slot = iota((8 * NZ, COLS), 0)
    slot_owner = (slot & 7) * NZ + (slot >> 3)
    mine = (slot_owner == owner_v[...]) & ((slot & 7) < ny)
    mine_f = mine.astype(F32)
    earlier = (iota((COLS, COLS), 0) < iota((COLS, COLS), 1)).astype(BF16)
    seen = matmul(mine_f.astype(BF16), earlier)
    rank = jnp.sum(mine_f * seen, axis=0, keepdims=True)
    target = rank + (dev * (COLS // n_dev)).astype(F32)
    put = (iota((COLS, COLS), 0).astype(F32) == target).astype(BF16)
    sums = jnp.concatenate(split3(jnp.where(mine, column_sum, 0.0)), axis=1)
    to_z[...] = matmul_nt(sums, jnp.concatenate([put, put, put], axis=1)).reshape(NZ, 8, COLS)
    from_z[me_z] = to_z[me_z]
    z_copies = [
        remote(to_z.at[lax.rem(me_z + k, NZ)], from_z.at[me_z], z_send.at[k], z_recv.at[k], z_peers[k - 1])
        for k in range(1, NZ)
    ]
    for copy in z_copies:
        copy.start()

    first_row = position * BPD

    def find(rows, limit, length, steps, wanted):
        found = jnp.int32(0)
        for step in steps:
            trial = found + step
            at = rows[jnp.minimum(trial, length) - 1]
            found = jnp.where((trial <= length) & (at <= wanted), trial, found)
        last = jnp.maximum(found - 1, 0)
        return last, jnp.where((found > 0) & (rows[last] == wanted), 1, 0)

    def find_own(r, carry):
        last, held = find(tile_rows, NT, NT, (128, 64, 32, 16, 8, 4, 2, 1), first_row + r)
        place[0, r] = last
        place[1, r] = held
        return carry

    lax.fori_loop(0, BPD, find_own, 0)
    for copy in index_copies:
        copy.wait()

    def find_got(r, carry):
        last, held = find(got_rows, SPILL, SPILL, (16, 8, 4, 2, 1), first_row + r)
        got_place[0, r] = last
        got_place[1, r] = held
        return carry

    lax.fori_loop(0, BPD, find_got, 0)

    load_tiles.wait()
    for copy in halo:
        copy.wait()

    for copy in spill[1:]:
        copy.start()

    first_col = first_row - REACH

    def own(t, run):
        block = jnp.clip(tile_cols[t] - first_col, 0, BPD + 2 * REACH - 1)
        term = matmul_nt(ext[block], own_tiles[t])
        goes_on = tile_rows[t] == tile_rows[jnp.maximum(t - 1, 0)]
        run = jnp.where(goes_on, run, 0.0) + term
        runs[t] = run
        return run

    lax.fori_loop(0, NT, own, jnp.zeros((NTR, BLK), F32), unroll=UNROLL)

    for r in range(BPD):
        lanes = slice(r * BLK, (r + 1) * BLK)
        updated[:, lanes] += jnp.where(place[1, r] == 1, runs[place[0, r]], 0.0)

    for copy in z_copies:
        copy.wait()
    over_z = from_z[0]
    for k in range(1, NZ):
        over_z += from_z[k]
    to_y[...] = over_z
    from_y[me_y] = over_z
    y_copies = [
        remote(to_y, from_y.at[me_y], y_send.at[k], y_recv.at[k], y_peers[k - 1]) for k in range(1, ny)
    ]
    for copy in y_copies:
        copy.start()

    run = jnp.zeros((NTR, BLK), F32)
    for c in range(TILE_CHUNKS):
        spill[c].wait()
        for s in range(c * TILES_SENT, (c + 1) * TILES_SENT):
            block = jnp.clip(got_cols[s] - first_col, 0, BPD + 2 * REACH - 1)
            term = matmul_nt(ext[block], got_tiles[s])
            goes_on = got_rows[s] == got_rows[max(s - 1, 0)]
            run = jnp.where(goes_on, run, 0.0) + term
            got_runs[s] = run

    for r in range(BPD):
        lanes = slice(r * BLK, (r + 1) * BLK)
        updated[:, lanes] += jnp.where(got_place[1, r] == 1, got_runs[got_place[0, r]], 0.0)

    for copy in y_copies:
        copy.wait()
    over_y = from_y[0]
    for k in range(1, ny):
        over_y += from_y[k]
    in_row = iota((8, COLS), 0) == me_y
    production[...] = jnp.sum(jnp.where(in_row, over_y, 0.0), axis=0)


def per_device(
    n_grp,
    n_dev,
    tracer,
    tile_rows,
    tile_cols,
    tile_values,
    level_counts,
    column_owner,
    half_saturation,
    growth_rate,
    uptake,
    graze_preference,
    graze_maximum,
):
    ny = n_dev // NZ
    anywhere = pl.BlockSpec(memory_space=pl.ANY)
    scalars = pl.BlockSpec(memory_space=pltpu.SMEM)
    vector = pl.BlockSpec(memory_space=pltpu.VMEM)
    dma = pltpu.SemaphoreType.DMA
    updated, production = pl.pallas_call(
        functools.partial(kernel, n_grp, n_dev),
        out_shape=(
            pltpu.VMEM((NTR, CD), F32),
            pltpu.VMEM((COLS,), F32),
        ),
        in_specs=[anywhere, scalars, scalars] + [anywhere] * 8,
        out_specs=(vector, vector),
        scratch_shapes=[
            pltpu.VMEM((NTR, CD), F32),
            pltpu.VMEM((BPD + 2 * REACH, NTR, BLK), BF16),
            pltpu.VMEM((NT, BLK, BLK), BF16),
            pltpu.VMEM((SPILL, BLK, BLK), BF16),
            pltpu.VMEM((NT, NTR, BLK), F32),
            pltpu.VMEM((SPILL, NTR, BLK), F32),
            pltpu.VMEM((1, COLS), jnp.int32),
            pltpu.VMEM((1, COLS), jnp.int32),
            pltpu.VMEM((1, NUT), F32),
            pltpu.VMEM((1, PLK), F32),
            pltpu.VMEM((NUT, PLK), F32),
            pltpu.VMEM((PLK, PLK), F32),
            pltpu.VMEM((1, PLK), F32),
            pltpu.VMEM((BPD, BLK), F32),
            pltpu.VMEM((BPD, BLK), F32),
            pltpu.VMEM((BPD, BLK), F32),
            pltpu.VMEM((BPD, BLK), F32),
            pltpu.VMEM((PLK, 3 * NUT), BF16),
            pltpu.VMEM((PLK, 3 * PLK), BF16),
            pltpu.VMEM((PLK, 3 * PLK), BF16),
            pltpu.VMEM((NUT, 3 * PLK), BF16),
            pltpu.VMEM((NZ, 8, COLS), F32),
            pltpu.VMEM((NZ, 8, COLS), F32),
            pltpu.VMEM((8, COLS), F32),
            pltpu.VMEM((ny, 8, COLS), F32),
            pltpu.SMEM((NT,), jnp.int32),
            pltpu.SMEM((NT,), jnp.int32),
            pltpu.SMEM((2, BPD), jnp.int32),
            pltpu.SMEM((2, BPD), jnp.int32),
            dma,
            dma,
            dma((SMALL,)),
            dma((2,)),
            dma((2,)),
            dma((TILE_CHUNKS,)),
            dma((TILE_CHUNKS,)),
            dma((4,)),
            dma((NZ,)),
            dma((NZ,)),
            dma((ny,)),
            dma((ny,)),
        ],
        compiler_params=pltpu.CompilerParams(
            collective_id=0, has_side_effects=True, vmem_limit_bytes=56 * 1024 * 1024
        ),
        name="plankton_step",
    )(
        tracer,
        tile_rows,
        tile_cols,
        tile_values,
        level_counts.reshape(1, COLS),
        column_owner.reshape(1, COLS),
        half_saturation.reshape(1, NUT),
        growth_rate.reshape(1, PLK),
        uptake.T,
        graze_preference,
        graze_maximum.reshape(1, PLK),
    )
    return updated, production


def solution(mesh):
    n_grp, n_dev = mesh.shape["grp"], mesh.shape["dev"]
    chain = P(("grp", "dev"))
    cells = P(None, ("grp", "dev"))
    return jax.shard_map(
        functools.partial(per_device, n_grp, n_dev),
        mesh=mesh,
        in_specs=(cells, chain, chain, P(("grp", "dev"), None, None), chain, chain, P(), P(), P(), P(), P()),
        out_specs=(cells, chain),
        check_vma=False,
    )
```

```python
import functools

import jax
import jax.numpy as jnp
from jax import lax
from jax.experimental import pallas as pl
from jax.experimental.pallas import tpu as pltpu
from jax.sharding import PartitionSpec as P

MESH = pl.DeviceIdType.MESH
F32 = jnp.float32
BF16 = jnp.bfloat16

NUT = 16
PLK = 64
NTR = 96
LEV = 32
COLS = 128
BLK = 128
BPD = 32
NT = 160
SPILL = 20
REACH = 16
CD = BPD * BLK
NZ = 8
WATER_DECAY = 0.03
SHADE_DECAY = 0.05
EFFICIENCY = 0.3
MORTALITY = 0.1
REMINERAL = 0.2
TIMESTEP = 0.5

TILE_CHUNKS = 5
TILES_SENT = SPILL // TILE_CHUNKS
GROUP = 256
UNROLL = 8
SMALL = 9


def iota(shape, dim):
    return lax.broadcasted_iota(jnp.int32, shape, dim)


def split2(x):
    high = x.astype(BF16)
    return high, (x - high.astype(F32)).astype(BF16)


def split3(x):
    high = x.astype(BF16)
    rest = x - high.astype(F32)
    middle = rest.astype(BF16)
    return high, middle, (rest - middle.astype(F32)).astype(BF16)


def weights3(w):
    high, low = split2(w)
    return jnp.concatenate([high, high, low], axis=1)


def data3(x):
    high, low = split2(x)
    return jnp.concatenate([high, low, high], axis=0)


def matmul(a, b):
    return jnp.dot(a, b, preferred_element_type=F32)


def matmul_nt(a, b):
    return lax.dot_general(a, b, (((1,), (1,)), ((), ())), preferred_element_type=F32)


def column_of(row):
    n = row.shape[1]
    return jnp.sum(jnp.where(iota((n, n), 0) == iota((n, n), 1), row, 0.0), axis=1, keepdims=True)


def kernel(
    n_grp,
    n_dev,
    tracer,
    rows_in,
    cols_in,
    tiles,
    levels,
    owner,
    half_saturation,
    growth_rate,
    uptake,
    preference,
    graze_maximum,
    updated,
    production,
    tr,
    ext,
    own_tiles,
    got_tiles,
    runs,
    got_runs,
    levels_v,
    owner_v,
    half_v,
    growth_v,
    uptake_v,
    preference_v,
    maximum_v,
    chl,
    wet,
    sun,
    grown,
    w_limit,
    w_food,
    w_graze,
    w_use,
    to_z,
    from_z,
    to_y,
    from_y,
    tile_rows,
    tile_cols,
    got_rows,
    got_cols,
    place,
    got_place,
    tracer_sem,
    tiles_sem,
    small_sem,
    halo_send,
    halo_recv,
    spill_send,
    spill_recv,
    rows_sem,
    z_send,
    z_recv,
    y_send,
    y_recv,
):
    ny = n_dev // NZ
    grp = lax.axis_index("grp")
    dev = lax.axis_index("dev")
    me_y = dev // NZ
    me_z = lax.rem(dev, NZ)
    position = grp * n_dev + dev
    count = n_grp * n_dev
    after = lax.rem(position + 1, count)
    before = lax.rem(position + count - 1, count)
    right = (after // n_dev, lax.rem(after, n_dev))
    left = (before // n_dev, lax.rem(before, n_dev))
    z_peers = [(grp, me_y * NZ + lax.rem(me_z + k, NZ)) for k in range(1, NZ)]
    y_peers = [(grp, lax.rem(me_y + k, ny) * NZ + me_z) for k in range(1, ny)]

    barrier = pltpu.get_barrier_semaphore()
    for peer in [left, right] + z_peers + y_peers:
        pl.semaphore_signal(barrier, inc=1, device_id=peer, device_id_type=MESH)

    load = pltpu.make_async_copy(tracer, tr, tracer_sem)
    load.start()
    small = [
        pltpu.make_async_copy(source, target, small_sem.at[i])
        for i, (source, target) in enumerate(
            [
                (levels, levels_v),
                (owner, owner_v),
                (half_saturation, half_v),
                (growth_rate, growth_v),
                (uptake, uptake_v),
                (preference, preference_v),
                (graze_maximum, maximum_v),
                (rows_in, tile_rows),
                (cols_in, tile_cols),
            ]
        )
    ]
    for copy in small:
        copy.start()
    load_tiles = pltpu.make_async_copy(tiles, own_tiles, tiles_sem)
    load_tiles.start()

    pl.semaphore_wait(barrier, 2 + (NZ - 1) + (ny - 1))

    def remote(source, target, send, recv, peer):
        return pltpu.make_async_remote_copy(
            src_ref=source,
            dst_ref=target,
            send_sem=send,
            recv_sem=recv,
            device_id=peer,
            device_id_type=MESH,
        )

    index_copies = [
        remote(rows_in, got_rows, rows_sem.at[0], rows_sem.at[1], left),
        remote(cols_in, got_cols, rows_sem.at[2], rows_sem.at[3], left),
    ]
    halo = [
        remote(
            ext.at[pl.ds(REACH, REACH)],
            ext.at[pl.ds(REACH + BPD, REACH)],
            halo_send.at[0],
            halo_recv.at[0],
            left,
        ),
        remote(
            ext.at[pl.ds(BPD, REACH)],
            ext.at[pl.ds(0, REACH)],
            halo_send.at[1],
            halo_recv.at[1],
            right,
        ),
    ]
    spill = [
        remote(
            (own_tiles if c else tiles).at[pl.ds(c * TILES_SENT, TILES_SENT)],
            got_tiles.at[pl.ds(c * TILES_SENT, TILES_SENT)],
            spill_send.at[c],
            spill_recv.at[c],
            left,
        )
        for c in range(TILE_CHUNKS)
    ]
    def round_blocks(first, blocks):
        for b in range(first, first + blocks):
            ext[REACH + b] = tr[:, b * BLK : (b + 1) * BLK].astype(BF16)

    for copy in spill[0:1]:
        copy.start()
    for copy in index_copies:
        copy.start()
    load.wait()
    round_blocks(0, REACH)
    halo[0].start()
    round_blocks(REACH, BPD - REACH)
    halo[1].start()

    for copy in small:
        copy.wait()
    w_limit[...] = weights3(uptake_v[...].T)
    w_food[...] = weights3(preference_v[...])
    w_graze[...] = weights3(preference_v[...].T)
    w_use[...] = weights3(uptake_v[...])
    half = column_of(half_v[...])
    growth_column = column_of(growth_v[...])
    maximum = column_of(maximum_v[...])

    column_row = iota((BPD, COLS), 1)
    pick_row = (column_row >> 2) == iota((BPD, COLS), 0)
    in_block = ((iota((COLS, BLK), 0) & 3) == (iota((COLS, BLK), 1) >> 5)).astype(BF16)
    level_row = jnp.where(pick_row, levels_v[...].astype(F32), 0.0).astype(BF16)
    wet_levels = matmul(level_row, in_block)
    depth = (iota((BPD, BLK), 1) & (LEV - 1)).astype(F32)
    wet_mask = (depth < wet_levels).astype(F32)
    wet[...] = wet_mask

    def sum_plankton(i, carry):
        lanes = pl.ds(pl.multiple_of(i * BLK, BLK), BLK)
        chl[pl.ds(i, 1), :] = jnp.sum(tr[NUT : NUT + PLK, lanes], axis=0, keepdims=True)
        return carry

    lax.fori_loop(0, BPD, sum_plankton, 0, unroll=4)
    upper_row, upper_col = iota((2 * BLK, BLK), 0) & (BLK - 1), iota((2 * BLK, BLK), 1)
    above = ((upper_row < upper_col) & ((upper_row >> 5) == (upper_col >> 5))).astype(BF16)
    chl_high, chl_low = split2(chl[...] * (1.0 / PLK) * wet_mask)
    shading = matmul(jnp.concatenate([chl_high, chl_low], axis=1), above)
    sun[...] = jnp.exp(-WATER_DECAY * depth - SHADE_DECAY * shading)

    fold_col = iota((NUT, 2 * PLK), 1) & (PLK - 1)
    fold = ((fold_col >> 2) == iota((NUT, 2 * PLK), 0)).astype(BF16)
    per_group = GROUP // BLK

    def row_of(ref, i):
        return jnp.concatenate([ref[pl.ds(i * per_group + h, 1), :] for h in range(per_group)], axis=1)

    def ecosystem(i, carry):
        lanes = pl.ds(pl.multiple_of(i * GROUP, GROUP), GROUP)
        mask = row_of(wet, i) * TIMESTEP
        light = row_of(sun, i)
        nutrient = tr[:NUT, lanes]
        plankton = tr[NUT : NUT + PLK, lanes]
        detritus = tr[NUT + PLK :, lanes]
        monod = nutrient / (nutrient + half)
        limitation = matmul(w_limit[...], data3(monod))
        capacity = growth_column * (light * plankton)
        growth = capacity * limitation
        food = matmul(w_food[...], data3(plankton))
        rate = maximum * plankton / (1.0 + food)
        eaten = rate * food
        grazed = plankton * matmul(w_graze[...], data3(rate))
        mortality = MORTALITY * plankton
        d_plankton = growth - grazed + EFFICIENCY * eaten - mortality
        use = matmul(w_use[...], data3(capacity))
        d_nutrient = REMINERAL * detritus - monod * use
        waste = (1.0 - EFFICIENCY) * eaten + mortality
        d_detritus = matmul(fold, jnp.concatenate(split2(waste), axis=0)) - REMINERAL * detritus
        updated[:NUT, lanes] = nutrient + mask * d_nutrient
        updated[NUT : NUT + PLK, lanes] = plankton + mask * d_plankton
        updated[NUT + PLK :, lanes] = detritus + mask * d_detritus
        total = jnp.sum(growth, axis=0, keepdims=True)
        for h in range(per_group):
            grown[pl.ds(i * per_group + h, 1), :] = total[:, h * BLK : (h + 1) * BLK]
        return carry

    lax.fori_loop(0, CD // GROUP, ecosystem, 0)

    summed = jnp.concatenate(split3(grown[...] * (1.0 / PLK) * wet_mask), axis=1)
    lane_row, lane_col = iota((3 * BLK, COLS), 0) & (BLK - 1), iota((3 * BLK, COLS), 1)
    gather_columns = ((lane_row >> 5) == (lane_col & 3)).astype(BF16)
    by_block = matmul(summed, gather_columns)
    column_sum = jnp.sum(jnp.where(pick_row, by_block, 0.0), axis=0, keepdims=True)
    slot = iota((8 * NZ, COLS), 0)
    slot_owner = (slot & 7) * NZ + (slot >> 3)
    mine = (slot_owner == owner_v[...]) & ((slot & 7) < ny)
    mine_f = mine.astype(F32)
    earlier = (iota((COLS, COLS), 0) < iota((COLS, COLS), 1)).astype(BF16)
    seen = matmul(mine_f.astype(BF16), earlier)
    rank = jnp.sum(mine_f * seen, axis=0, keepdims=True)
    target = rank + (dev * (COLS // n_dev)).astype(F32)
    put = (iota((COLS, COLS), 0).astype(F32) == target).astype(BF16)
    sums = jnp.concatenate(split3(jnp.where(mine, column_sum, 0.0)), axis=1)
    to_z[...] = matmul_nt(sums, jnp.concatenate([put, put, put], axis=1)).reshape(NZ, 8, COLS)
    from_z[me_z] = to_z[me_z]
    z_copies = [
        remote(to_z.at[lax.rem(me_z + k, NZ)], from_z.at[me_z], z_send.at[k], z_recv.at[k], z_peers[k - 1])
        for k in range(1, NZ)
    ]
    for copy in z_copies:
        copy.start()

    load_tiles.wait()
    for copy in spill[1:3]:
        copy.start()
    first_row = position * BPD

    def find(rows, limit, length, steps, wanted):
        found = jnp.int32(0)
        for step in steps:
            trial = found + step
            at = rows[jnp.minimum(trial, length) - 1]
            found = jnp.where((trial <= length) & (at <= wanted), trial, found)
        last = jnp.maximum(found - 1, 0)
        return last, jnp.where((found > 0) & (rows[last] == wanted), 1, 0)

    def find_own(r, carry):
        last, held = find(tile_rows, NT, NT, (128, 64, 32, 16, 8, 4, 2, 1), first_row + r)
        place[0, r] = last
        place[1, r] = held
        return carry

    lax.fori_loop(0, BPD, find_own, 0)
    for copy in index_copies:
        copy.wait()

    def find_got(r, carry):
        last, held = find(got_rows, SPILL, SPILL, (16, 8, 4, 2, 1), first_row + r)
        got_place[0, r] = last
        got_place[1, r] = held
        return carry

    lax.fori_loop(0, BPD, find_got, 0)

    halo[0].wait_send()

    halo[0].wait_recv()
    halo[1].wait()

    first_col = first_row - REACH

    def own(t, run):
        block = jnp.clip(tile_cols[t] - first_col, 0, BPD + 2 * REACH - 1)
        term = matmul_nt(ext[block], own_tiles[t])
        goes_on = tile_rows[t] == tile_rows[jnp.maximum(t - 1, 0)]
        run = jnp.where(goes_on, run, 0.0) + term
        runs[t] = run
        return run

    run = lax.fori_loop(0, 80, own, jnp.zeros((NTR, BLK), F32), unroll=UNROLL)

    for copy in z_copies:
        copy.wait()
    over_z = from_z[0]
    for k in range(1, NZ):
        over_z += from_z[k]
    to_y[...] = over_z
    from_y[me_y] = over_z
    y_copies = [
        remote(to_y, from_y.at[me_y], y_send.at[k], y_recv.at[k], y_peers[k - 1]) for k in range(1, ny)
    ]
    for copy in y_copies:
        copy.start()

    for copy in spill[3:]:
        copy.start()

    lax.fori_loop(80, NT, own, run, unroll=UNROLL)

    for r in range(BPD):
        lanes = slice(r * BLK, (r + 1) * BLK)
        updated[:, lanes] += jnp.where(place[1, r] == 1, runs[place[0, r]], 0.0)

    run = jnp.zeros((NTR, BLK), F32)
    for c in range(TILE_CHUNKS):
        spill[c].wait()
        for s in range(c * TILES_SENT, (c + 1) * TILES_SENT):
            block = jnp.clip(got_cols[s] - first_col, 0, BPD + 2 * REACH - 1)
            term = matmul_nt(ext[block], got_tiles[s])
            goes_on = got_rows[s] == got_rows[max(s - 1, 0)]
            run = jnp.where(goes_on, run, 0.0) + term
            got_runs[s] = run

    for r in range(BPD):
        lanes = slice(r * BLK, (r + 1) * BLK)
        updated[:, lanes] += jnp.where(got_place[1, r] == 1, got_runs[got_place[0, r]], 0.0)

    for copy in y_copies:
        copy.wait()
    over_y = from_y[0]
    for k in range(1, ny):
        over_y += from_y[k]
    in_row = iota((8, COLS), 0) == me_y
    production[...] = jnp.sum(jnp.where(in_row, over_y, 0.0), axis=0)


def write_out(updated, production, updated_out, production_out, sem):
    copies = [
        pltpu.make_async_copy(updated, updated_out, sem.at[0]),
        pltpu.make_async_copy(production, production_out, sem.at[1]),
    ]
    for copy in copies:
        copy.start()
    for copy in copies:
        copy.wait()


def per_device(
    n_grp,
    n_dev,
    tracer,
    tile_rows,
    tile_cols,
    tile_values,
    level_counts,
    column_owner,
    half_saturation,
    growth_rate,
    uptake,
    graze_preference,
    graze_maximum,
):
    ny = n_dev // NZ
    anywhere = pl.BlockSpec(memory_space=pl.ANY)
    vector = pl.BlockSpec(memory_space=pltpu.VMEM)
    dma = pltpu.SemaphoreType.DMA
    updated, production = pl.pallas_call(
        functools.partial(kernel, n_grp, n_dev),
        out_shape=(
            pltpu.VMEM((NTR, CD), F32),
            pltpu.VMEM((COLS,), F32),
        ),
        in_specs=[anywhere] * 11,
        out_specs=(vector, vector),
        scratch_shapes=[
            pltpu.VMEM((NTR, CD), F32),
            pltpu.VMEM((BPD + 2 * REACH, NTR, BLK), BF16),
            pltpu.VMEM((NT, BLK, BLK), BF16),
            pltpu.VMEM((SPILL, BLK, BLK), BF16),
            pltpu.VMEM((NT, NTR, BLK), F32),
            pltpu.VMEM((SPILL, NTR, BLK), F32),
            pltpu.VMEM((1, COLS), jnp.int32),
            pltpu.VMEM((1, COLS), jnp.int32),
            pltpu.VMEM((1, NUT), F32),
            pltpu.VMEM((1, PLK), F32),
            pltpu.VMEM((NUT, PLK), F32),
            pltpu.VMEM((PLK, PLK), F32),
            pltpu.VMEM((1, PLK), F32),
            pltpu.VMEM((BPD, BLK), F32),
            pltpu.VMEM((BPD, BLK), F32),
            pltpu.VMEM((BPD, BLK), F32),
            pltpu.VMEM((BPD, BLK), F32),
            pltpu.VMEM((PLK, 3 * NUT), BF16),
            pltpu.VMEM((PLK, 3 * PLK), BF16),
            pltpu.VMEM((PLK, 3 * PLK), BF16),
            pltpu.VMEM((NUT, 3 * PLK), BF16),
            pltpu.VMEM((NZ, 8, COLS), F32),
            pltpu.VMEM((NZ, 8, COLS), F32),
            pltpu.VMEM((8, COLS), F32),
            pltpu.VMEM((ny, 8, COLS), F32),
            pltpu.SMEM((NT,), jnp.int32),
            pltpu.SMEM((NT,), jnp.int32),
            pltpu.SMEM((NT,), jnp.int32),
            pltpu.SMEM((NT,), jnp.int32),
            pltpu.SMEM((2, BPD), jnp.int32),
            pltpu.SMEM((2, BPD), jnp.int32),
            dma,
            dma,
            dma((SMALL,)),
            dma((2,)),
            dma((2,)),
            dma((TILE_CHUNKS,)),
            dma((TILE_CHUNKS,)),
            dma((4,)),
            dma((NZ,)),
            dma((NZ,)),
            dma((ny,)),
            dma((ny,)),
        ],
        compiler_params=pltpu.CompilerParams(
            collective_id=0, has_side_effects=True, vmem_limit_bytes=56 * 1024 * 1024
        ),
        name="plankton_step",
    )(
        tracer,
        tile_rows,
        tile_cols,
        tile_values,
        level_counts.reshape(1, COLS),
        column_owner.reshape(1, COLS),
        half_saturation.reshape(1, NUT),
        growth_rate.reshape(1, PLK),
        uptake.T,
        graze_preference,
        graze_maximum.reshape(1, PLK),
    )
    return pl.pallas_call(
        write_out,
        out_shape=(
            jax.ShapeDtypeStruct((NTR, CD), F32),
            jax.ShapeDtypeStruct((COLS,), F32),
        ),
        in_specs=(vector, vector),
        out_specs=(anywhere, anywhere),
        scratch_shapes=[dma((2,))],
        compiler_params=pltpu.CompilerParams(vmem_limit_bytes=1024 * 1024),
        name="write_out",
    )(updated, production)


def solution(mesh):
    n_grp, n_dev = mesh.shape["grp"], mesh.shape["dev"]
    chain = P(("grp", "dev"))
    cells = P(None, ("grp", "dev"))
    return jax.shard_map(
        functools.partial(per_device, n_grp, n_dev),
        mesh=mesh,
        in_specs=(cells, chain, chain, P(("grp", "dev"), None, None), chain, chain, P(), P(), P(), P(), P()),
        out_specs=(cells, chain),
        check_vma=False,
    )
```

```python
import functools

import jax
import jax.numpy as jnp
from jax import lax
from jax.experimental import pallas as pl
from jax.experimental.pallas import tpu as pltpu
from jax.sharding import PartitionSpec as P

MESH = pl.DeviceIdType.MESH
F32 = jnp.float32
BF16 = jnp.bfloat16

NUT = 16
PLK = 64
NTR = 96
LEV = 32
COLS = 128
BLK = 128
BPD = 32
NT = 160
SPILL = 20
REACH = 16
CD = BPD * BLK
NZ = 8
WATER_DECAY = 0.03
SHADE_DECAY = 0.05
EFFICIENCY = 0.3
MORTALITY = 0.1
REMINERAL = 0.2
TIMESTEP = 0.5

TILE_CHUNKS = 5
TILES_SENT = SPILL // TILE_CHUNKS
GROUP = 256
UNROLL = 8
SMALL = 9


def iota(shape, dim):
    return lax.broadcasted_iota(jnp.int32, shape, dim)


def split2(x):
    high = x.astype(BF16)
    return high, (x - high.astype(F32)).astype(BF16)


def split3(x):
    high = x.astype(BF16)
    rest = x - high.astype(F32)
    middle = rest.astype(BF16)
    return high, middle, (rest - middle.astype(F32)).astype(BF16)


def weights3(w):
    high, low = split2(w)
    return jnp.concatenate([high, high, low], axis=1)


def data3(x):
    high, low = split2(x)
    return jnp.concatenate([high, low, high], axis=0)


def matmul(a, b):
    return jnp.dot(a, b, preferred_element_type=F32)


def matmul_nt(a, b):
    return lax.dot_general(a, b, (((1,), (1,)), ((), ())), preferred_element_type=F32)


def column_of(row):
    n = row.shape[1]
    return jnp.sum(jnp.where(iota((n, n), 0) == iota((n, n), 1), row, 0.0), axis=1, keepdims=True)


def kernel(
    n_grp,
    n_dev,
    tracer,
    rows_in,
    cols_in,
    tiles,
    levels,
    owner,
    half_saturation,
    growth_rate,
    uptake,
    preference,
    graze_maximum,
    updated,
    production,
    tr,
    ext,
    own_tiles,
    got_tiles,
    runs,
    got_runs,
    levels_v,
    owner_v,
    half_v,
    growth_v,
    uptake_v,
    preference_v,
    maximum_v,
    chl,
    wet,
    sun,
    grown,
    w_limit,
    w_food,
    w_graze,
    w_use,
    to_z,
    from_z,
    to_y,
    from_y,
    tile_rows,
    tile_cols,
    got_rows,
    got_cols,
    place,
    got_place,
    tracer_sem,
    tiles_sem,
    small_sem,
    halo_send,
    halo_recv,
    spill_send,
    spill_recv,
    rows_sem,
    z_send,
    z_recv,
    y_send,
    y_recv,
):
    ny = n_dev // NZ
    share = COLS // n_dev
    grp = lax.axis_index("grp")
    dev = lax.axis_index("dev")
    me_y = dev // NZ
    me_z = lax.rem(dev, NZ)
    position = grp * n_dev + dev
    count = n_grp * n_dev
    after = lax.rem(position + 1, count)
    before = lax.rem(position + count - 1, count)
    right = (after // n_dev, lax.rem(after, n_dev))
    left = (before // n_dev, lax.rem(before, n_dev))
    z_peers = [(grp, me_y * NZ + lax.rem(me_z + k, NZ)) for k in range(1, NZ)]
    y_peers = [(grp, lax.rem(me_y + k, ny) * NZ + me_z) for k in range(1, ny)]

    barrier = pltpu.get_barrier_semaphore()
    for peer in [left, right] + z_peers + y_peers:
        pl.semaphore_signal(barrier, inc=1, device_id=peer, device_id_type=MESH)

    load = pltpu.make_async_copy(tracer, tr, tracer_sem)
    load.start()
    small = [
        pltpu.make_async_copy(source, target, small_sem.at[i])
        for i, (source, target) in enumerate(
            [
                (levels, levels_v),
                (owner, owner_v),
                (half_saturation, half_v),
                (growth_rate, growth_v),
                (uptake, uptake_v),
                (preference, preference_v),
                (graze_maximum, maximum_v),
                (rows_in, tile_rows),
                (cols_in, tile_cols),
            ]
        )
    ]
    for copy in small:
        copy.start()
    load_tiles = pltpu.make_async_copy(tiles, own_tiles, tiles_sem)
    load_tiles.start()

    pl.semaphore_wait(barrier, 2 + (NZ - 1) + (ny - 1))

    def remote(source, target, send, recv, peer):
        return pltpu.make_async_remote_copy(
            src_ref=source,
            dst_ref=target,
            send_sem=send,
            recv_sem=recv,
            device_id=peer,
            device_id_type=MESH,
        )

    index_copies = [
        remote(rows_in, got_rows, rows_sem.at[0], rows_sem.at[1], left),
        remote(cols_in, got_cols, rows_sem.at[2], rows_sem.at[3], left),
    ]
    halo = [
        remote(
            ext.at[pl.ds(REACH, REACH)],
            ext.at[pl.ds(REACH + BPD, REACH)],
            halo_send.at[0],
            halo_recv.at[0],
            left,
        ),
        remote(
            ext.at[pl.ds(BPD, REACH)],
            ext.at[pl.ds(0, REACH)],
            halo_send.at[1],
            halo_recv.at[1],
            right,
        ),
    ]
    spill = [
        remote(
            (own_tiles if c else tiles).at[pl.ds(c * TILES_SENT, TILES_SENT)],
            got_tiles.at[pl.ds(c * TILES_SENT, TILES_SENT)],
            spill_send.at[c],
            spill_recv.at[c],
            left,
        )
        for c in range(TILE_CHUNKS)
    ]
    def round_blocks(first, blocks):
        for b in range(first, first + blocks):
            ext[REACH + b] = tr[:, b * BLK : (b + 1) * BLK].astype(BF16)

    for copy in spill[0:1]:
        copy.start()
    load.wait()
    round_blocks(0, REACH)
    halo[0].start()
    round_blocks(REACH, BPD - REACH)
    halo[1].start()
    for copy in index_copies:
        copy.start()

    for copy in small:
        copy.wait()
    w_limit[...] = weights3(uptake_v[...].T)
    w_food[...] = weights3(preference_v[...])
    w_graze[...] = weights3(preference_v[...].T)
    w_use[...] = weights3(uptake_v[...])
    half = column_of(half_v[...])
    growth_column = column_of(growth_v[...])
    maximum = column_of(maximum_v[...])

    column_row = iota((BPD, COLS), 1)
    pick_row = (column_row >> 2) == iota((BPD, COLS), 0)
    in_block = ((iota((COLS, BLK), 0) & 3) == (iota((COLS, BLK), 1) >> 5)).astype(BF16)
    level_row = jnp.where(pick_row, levels_v[...].astype(F32), 0.0).astype(BF16)
    wet_levels = matmul(level_row, in_block)
    depth = (iota((BPD, BLK), 1) & (LEV - 1)).astype(F32)
    wet_mask = (depth < wet_levels).astype(F32)
    wet[...] = wet_mask

    def sum_plankton(i, carry):
        lanes = pl.ds(pl.multiple_of(i * BLK, BLK), BLK)
        chl[pl.ds(i, 1), :] = jnp.sum(tr[NUT : NUT + PLK, lanes], axis=0, keepdims=True)
        return carry

    lax.fori_loop(0, BPD, sum_plankton, 0, unroll=4)
    upper_row, upper_col = iota((2 * BLK, BLK), 0) & (BLK - 1), iota((2 * BLK, BLK), 1)
    above = ((upper_row < upper_col) & ((upper_row >> 5) == (upper_col >> 5))).astype(BF16)
    chl_high, chl_low = split2(chl[...] * (1.0 / PLK) * wet_mask)
    shading = matmul(jnp.concatenate([chl_high, chl_low], axis=1), above)
    sun[...] = jnp.exp(-WATER_DECAY * depth - SHADE_DECAY * shading)

    fold_col = iota((NUT, 2 * PLK), 1) & (PLK - 1)
    fold = ((fold_col >> 2) == iota((NUT, 2 * PLK), 0)).astype(BF16)
    per_group = GROUP // BLK

    def row_of(ref, i):
        return jnp.concatenate([ref[pl.ds(i * per_group + h, 1), :] for h in range(per_group)], axis=1)

    def ecosystem(i, carry):
        lanes = pl.ds(pl.multiple_of(i * GROUP, GROUP), GROUP)
        mask = row_of(wet, i) * TIMESTEP
        light = row_of(sun, i)
        nutrient = tr[:NUT, lanes]
        plankton = tr[NUT : NUT + PLK, lanes]
        detritus = tr[NUT + PLK :, lanes]
        monod = nutrient / (nutrient + half)
        limitation = matmul(w_limit[...], data3(monod))
        capacity = growth_column * (light * plankton)
        growth = capacity * limitation
        food = matmul(w_food[...], data3(plankton))
        rate = maximum * plankton / (1.0 + food)
        eaten = rate * food
        grazed = plankton * matmul(w_graze[...], data3(rate))
        mortality = MORTALITY * plankton
        d_plankton = growth - grazed + EFFICIENCY * eaten - mortality
        use = matmul(w_use[...], data3(capacity))
        d_nutrient = REMINERAL * detritus - monod * use
        waste = (1.0 - EFFICIENCY) * eaten + mortality
        d_detritus = matmul(fold, jnp.concatenate(split2(waste), axis=0)) - REMINERAL * detritus
        updated[:NUT, lanes] = nutrient + mask * d_nutrient
        updated[NUT : NUT + PLK, lanes] = plankton + mask * d_plankton
        updated[NUT + PLK :, lanes] = detritus + mask * d_detritus
        total = jnp.sum(growth, axis=0, keepdims=True)
        for h in range(per_group):
            grown[pl.ds(i * per_group + h, 1), :] = total[:, h * BLK : (h + 1) * BLK]
        return carry

    lax.fori_loop(0, CD // GROUP, ecosystem, 0)

    summed = jnp.concatenate(split3(grown[...] * (1.0 / PLK) * wet_mask), axis=1)
    lane_row, lane_col = iota((3 * BLK, COLS), 0) & (BLK - 1), iota((3 * BLK, COLS), 1)
    gather_columns = ((lane_row >> 5) == (lane_col & 3)).astype(BF16)
    by_block = matmul(summed, gather_columns)
    column_sum = jnp.sum(jnp.where(pick_row, by_block, 0.0), axis=0, keepdims=True)
    owners = owner_v[...]
    mine = (iota((n_dev, COLS), 0) == owners).astype(F32)
    earlier = (iota((COLS, COLS), 0) < iota((COLS, COLS), 1)).astype(BF16)
    seen = matmul(mine.astype(BF16), earlier)
    rank = jnp.sum(mine * seen, axis=0, keepdims=True)
    target = rank + ((owners >> 3) * share + me_z * (ny * share)).astype(F32)
    put = (iota((COLS, COLS), 0).astype(F32) == target).astype(BF16)
    to_this_z = (owners & (NZ - 1)) == iota((NZ, COLS), 0)
    sums = jnp.concatenate(split3(jnp.where(to_this_z, column_sum, 0.0)), axis=1)
    to_z[...] = matmul_nt(sums, jnp.concatenate([put, put, put], axis=1)).reshape(NZ, 1, COLS)
    from_z[me_z] = to_z[me_z]
    z_copies = [
        remote(to_z.at[lax.rem(me_z + k, NZ)], from_z.at[me_z], z_send.at[k], z_recv.at[k], z_peers[k - 1])
        for k in range(1, NZ)
    ]
    for copy in z_copies:
        copy.start()

    load_tiles.wait()
    for copy in spill[1:3]:
        copy.start()
    first_row = position * BPD

    def find(rows, limit, length, steps, wanted):
        found = jnp.int32(0)
        for step in steps:
            trial = found + step
            at = rows[jnp.minimum(trial, length) - 1]
            found = jnp.where((trial <= length) & (at <= wanted), trial, found)
        last = jnp.maximum(found - 1, 0)
        return last, jnp.where((found > 0) & (rows[last] == wanted), 1, 0)

    def find_own(r, carry):
        last, held = find(tile_rows, NT, NT, (128, 64, 32, 16, 8, 4, 2, 1), first_row + r)
        place[0, r] = last
        place[1, r] = held
        return carry

    lax.fori_loop(0, BPD, find_own, 0)
    for copy in index_copies:
        copy.wait()

    def find_got(r, carry):
        last, held = find(got_rows, SPILL, SPILL, (16, 8, 4, 2, 1), first_row + r)
        got_place[0, r] = last
        got_place[1, r] = held
        return carry

    lax.fori_loop(0, BPD, find_got, 0)

    halo[0].wait_send()

    halo[0].wait_recv()
    halo[1].wait()

    first_col = first_row - REACH

    def own(t, run):
        block = jnp.clip(tile_cols[t] - first_col, 0, BPD + 2 * REACH - 1)
        term = matmul_nt(ext[block], own_tiles[t])
        goes_on = tile_rows[t] == tile_rows[jnp.maximum(t - 1, 0)]
        run = jnp.where(goes_on, run, 0.0) + term
        runs[t] = run
        return run

    run = lax.fori_loop(0, 80, own, jnp.zeros((NTR, BLK), F32), unroll=UNROLL)

    for copy in z_copies:
        copy.wait()
    over_z = from_z[0]
    for k in range(1, NZ):
        over_z += from_z[k]
    to_y[...] = over_z
    from_y[me_y] = over_z
    y_copies = [
        remote(to_y, from_y.at[me_y], y_send.at[k], y_recv.at[k], y_peers[k - 1]) for k in range(1, ny)
    ]
    for copy in y_copies:
        copy.start()

    for copy in spill[3:]:
        copy.start()

    lax.fori_loop(80, NT, own, run, unroll=UNROLL)

    for r in range(BPD):
        lanes = slice(r * BLK, (r + 1) * BLK)
        updated[:, lanes] += jnp.where(place[1, r] == 1, runs[place[0, r]], 0.0)

    run = jnp.zeros((NTR, BLK), F32)
    for c in range(TILE_CHUNKS):
        spill[c].wait()
        for s in range(c * TILES_SENT, (c + 1) * TILES_SENT):
            block = jnp.clip(got_cols[s] - first_col, 0, BPD + 2 * REACH - 1)
            term = matmul_nt(ext[block], got_tiles[s])
            goes_on = got_rows[s] == got_rows[max(s - 1, 0)]
            run = jnp.where(goes_on, run, 0.0) + term
            got_runs[s] = run

    for r in range(BPD):
        lanes = slice(r * BLK, (r + 1) * BLK)
        updated[:, lanes] += jnp.where(got_place[1, r] == 1, got_runs[got_place[0, r]], 0.0)

    for copy in y_copies:
        copy.wait()
    rows = jnp.concatenate([from_y[k] for k in range(ny)] + [jnp.zeros((8 - ny, COLS), F32)], axis=0)
    out_row, out_lane = iota((3 * COLS, COLS), 0) & (COLS - 1), iota((3 * COLS, COLS), 1)
    source = ((out_lane // share) & (NZ - 1)) * (ny * share) + me_y * share + (out_lane & (share - 1))
    moved = matmul(jnp.concatenate(split3(rows), axis=1), (out_row == source).astype(BF16))
    from_row = iota((8, COLS), 1) // (NZ * share) == iota((8, COLS), 0)
    production[...] = jnp.sum(jnp.where(from_row, moved, 0.0), axis=0)


def write_out(updated, production, updated_out, production_out, sem):
    copies = [
        pltpu.make_async_copy(updated, updated_out, sem.at[0]),
        pltpu.make_async_copy(production, production_out, sem.at[1]),
    ]
    for copy in copies:
        copy.start()
    for copy in copies:
        copy.wait()


def per_device(
    n_grp,
    n_dev,
    tracer,
    tile_rows,
    tile_cols,
    tile_values,
    level_counts,
    column_owner,
    half_saturation,
    growth_rate,
    uptake,
    graze_preference,
    graze_maximum,
):
    ny = n_dev // NZ
    anywhere = pl.BlockSpec(memory_space=pl.ANY)
    vector = pl.BlockSpec(memory_space=pltpu.VMEM)
    dma = pltpu.SemaphoreType.DMA
    updated, production = pl.pallas_call(
        functools.partial(kernel, n_grp, n_dev),
        out_shape=(
            pltpu.VMEM((NTR, CD), F32),
            pltpu.VMEM((COLS,), F32),
        ),
        in_specs=[anywhere] * 11,
        out_specs=(vector, vector),
        scratch_shapes=[
            pltpu.VMEM((NTR, CD), F32),
            pltpu.VMEM((BPD + 2 * REACH, NTR, BLK), BF16),
            pltpu.VMEM((NT, BLK, BLK), BF16),
            pltpu.VMEM((SPILL, BLK, BLK), BF16),
            pltpu.VMEM((NT, NTR, BLK), F32),
            pltpu.VMEM((SPILL, NTR, BLK), F32),
            pltpu.VMEM((1, COLS), jnp.int32),
            pltpu.VMEM((1, COLS), jnp.int32),
            pltpu.VMEM((1, NUT), F32),
            pltpu.VMEM((1, PLK), F32),
            pltpu.VMEM((NUT, PLK), F32),
            pltpu.VMEM((PLK, PLK), F32),
            pltpu.VMEM((1, PLK), F32),
            pltpu.VMEM((BPD, BLK), F32),
            pltpu.VMEM((BPD, BLK), F32),
            pltpu.VMEM((BPD, BLK), F32),
            pltpu.VMEM((BPD, BLK), F32),
            pltpu.VMEM((PLK, 3 * NUT), BF16),
            pltpu.VMEM((PLK, 3 * PLK), BF16),
            pltpu.VMEM((PLK, 3 * PLK), BF16),
            pltpu.VMEM((NUT, 3 * PLK), BF16),
            pltpu.VMEM((NZ, 1, COLS), F32),
            pltpu.VMEM((NZ, 1, COLS), F32),
            pltpu.VMEM((1, COLS), F32),
            pltpu.VMEM((ny, 1, COLS), F32),
            pltpu.SMEM((NT,), jnp.int32),
            pltpu.SMEM((NT,), jnp.int32),
            pltpu.SMEM((NT,), jnp.int32),
            pltpu.SMEM((NT,), jnp.int32),
            pltpu.SMEM((2, BPD), jnp.int32),
            pltpu.SMEM((2, BPD), jnp.int32),
            dma,
            dma,
            dma((SMALL,)),
            dma((2,)),
            dma((2,)),
            dma((TILE_CHUNKS,)),
            dma((TILE_CHUNKS,)),
            dma((4,)),
            dma((NZ,)),
            dma((NZ,)),
            dma((ny,)),
            dma((ny,)),
        ],
        compiler_params=pltpu.CompilerParams(
            collective_id=0, has_side_effects=True, vmem_limit_bytes=56 * 1024 * 1024
        ),
        name="plankton_step",
    )(
        tracer,
        tile_rows,
        tile_cols,
        tile_values,
        level_counts.reshape(1, COLS),
        column_owner.reshape(1, COLS),
        half_saturation.reshape(1, NUT),
        growth_rate.reshape(1, PLK),
        uptake.T,
        graze_preference,
        graze_maximum.reshape(1, PLK),
    )
    return pl.pallas_call(
        write_out,
        out_shape=(
            jax.ShapeDtypeStruct((NTR, CD), F32),
            jax.ShapeDtypeStruct((COLS,), F32),
        ),
        in_specs=(vector, vector),
        out_specs=(anywhere, anywhere),
        scratch_shapes=[dma((2,))],
        compiler_params=pltpu.CompilerParams(vmem_limit_bytes=1024 * 1024),
        name="write_out",
    )(updated, production)


def solution(mesh):
    n_grp, n_dev = mesh.shape["grp"], mesh.shape["dev"]
    chain = P(("grp", "dev"))
    cells = P(None, ("grp", "dev"))
    return jax.shard_map(
        functools.partial(per_device, n_grp, n_dev),
        mesh=mesh,
        in_specs=(cells, chain, chain, P(("grp", "dev"), None, None), chain, chain, P(), P(), P(), P(), P()),
        out_specs=(cells, chain),
        check_vma=False,
    )
```

```python
import functools

import jax
import jax.numpy as jnp
from jax import lax
from jax.experimental import pallas as pl
from jax.experimental.pallas import tpu as pltpu
from jax.sharding import PartitionSpec as P

MESH = pl.DeviceIdType.MESH
F32 = jnp.float32
BF16 = jnp.bfloat16

NUT = 16
PLK = 64
NTR = 96
LEV = 32
COLS = 128
BLK = 128
BPD = 32
NT = 160
SPILL = 20
REACH = 16
CD = BPD * BLK
NZ = 8
WATER_DECAY = 0.03
SHADE_DECAY = 0.05
EFFICIENCY = 0.3
MORTALITY = 0.1
REMINERAL = 0.2
TIMESTEP = 0.5

BOUNDS = (0, 4, 12, 17, 19)
RELAYED = 1
TILE_CHUNKS = len(BOUNDS) - 1
GROUP = 256
UNROLL = 8
SMALL = 9


def iota(shape, dim):
    return lax.broadcasted_iota(jnp.int32, shape, dim)


def split2(x):
    high = x.astype(BF16)
    return high, (x - high.astype(F32)).astype(BF16)


def split3(x):
    high = x.astype(BF16)
    rest = x - high.astype(F32)
    middle = rest.astype(BF16)
    return high, middle, (rest - middle.astype(F32)).astype(BF16)


def weights3(w):
    high, low = split2(w)
    return jnp.concatenate([high, high, low], axis=1)


def data3(x):
    high, low = split2(x)
    return jnp.concatenate([high, low, high], axis=0)


def matmul(a, b):
    return jnp.dot(a, b, preferred_element_type=F32)


def matmul_nt(a, b):
    return lax.dot_general(a, b, (((1,), (1,)), ((), ())), preferred_element_type=F32)


def column_of(row):
    n = row.shape[1]
    return jnp.sum(jnp.where(iota((n, n), 0) == iota((n, n), 1), row, 0.0), axis=1, keepdims=True)


def kernel(
    n_grp,
    n_dev,
    tracer,
    rows_in,
    cols_in,
    tiles,
    levels,
    owner,
    half_saturation,
    growth_rate,
    uptake,
    preference,
    graze_maximum,
    updated,
    production,
    tr,
    ext,
    own_tiles,
    got_tiles,
    runs,
    got_runs,
    levels_v,
    owner_v,
    half_v,
    growth_v,
    uptake_v,
    preference_v,
    maximum_v,
    chl,
    wet,
    sun,
    grown,
    w_limit,
    w_food,
    w_graze,
    w_use,
    to_z,
    from_z,
    to_y,
    from_y,
    tile_rows,
    tile_cols,
    got_rows,
    got_cols,
    place,
    got_place,
    tracer_sem,
    tiles_sem,
    small_sem,
    halo_send,
    halo_recv,
    spill_send,
    spill_recv,
    rows_sem,
    z_send,
    z_recv,
    y_send,
    y_recv,
    passing,
    hop_send,
    hop_recv,
):
    ny = n_dev // NZ
    share = COLS // n_dev
    grp = lax.axis_index("grp")
    dev = lax.axis_index("dev")
    me_y = dev // NZ
    me_z = lax.rem(dev, NZ)
    position = grp * n_dev + dev
    count = n_grp * n_dev
    after = lax.rem(position + 1, count)
    before = lax.rem(position + count - 1, count)
    right = (after // n_dev, lax.rem(after, n_dev))
    left = (before // n_dev, lax.rem(before, n_dev))
    z_peers = [(grp, me_y * NZ + lax.rem(me_z + k, NZ)) for k in range(1, NZ)]
    y_peers = [(grp, lax.rem(me_y + k, ny) * NZ + me_z) for k in range(1, ny)]

    third = (grp, me_y * NZ + lax.rem(me_z + 3, NZ))
    origin = me_y * NZ + lax.rem(me_z + 2, NZ)
    last_to = (grp, lax.rem(origin + n_dev - 1, n_dev))
    sender = lax.rem(dev + 1, n_dev)
    last_from = (grp, (sender // NZ) * NZ + lax.rem(lax.rem(sender, NZ) + NZ - 2, NZ))
    barrier = pltpu.get_barrier_semaphore()
    for peer in [left, right, last_from] + z_peers + y_peers:
        pl.semaphore_signal(barrier, inc=1, device_id=peer, device_id_type=MESH)

    load = pltpu.make_async_copy(tracer, tr, tracer_sem)
    load.start()
    small = [
        pltpu.make_async_copy(source, target, small_sem.at[i])
        for i, (source, target) in enumerate(
            [
                (levels, levels_v),
                (owner, owner_v),
                (half_saturation, half_v),
                (growth_rate, growth_v),
                (uptake, uptake_v),
                (preference, preference_v),
                (graze_maximum, maximum_v),
                (rows_in, tile_rows),
                (cols_in, tile_cols),
            ]
        )
    ]
    for copy in small:
        copy.start()
    load_tiles = pltpu.make_async_copy(tiles, own_tiles, tiles_sem)
    load_tiles.start()

    pl.semaphore_wait(barrier, 3 + (NZ - 1) + (ny - 1))

    def remote(source, target, send, recv, peer):
        return pltpu.make_async_remote_copy(
            src_ref=source,
            dst_ref=target,
            send_sem=send,
            recv_sem=recv,
            device_id=peer,
            device_id_type=MESH,
        )

    index_copies = [
        remote(rows_in, got_rows, rows_sem.at[0], rows_sem.at[1], left),
        remote(cols_in, got_cols, rows_sem.at[2], rows_sem.at[3], left),
    ]
    halo = [
        remote(
            ext.at[pl.ds(REACH, REACH)],
            ext.at[pl.ds(REACH + BPD, REACH)],
            halo_send.at[0],
            halo_recv.at[0],
            left,
        ),
        remote(
            ext.at[pl.ds(BPD, REACH)],
            ext.at[pl.ds(0, REACH)],
            halo_send.at[1],
            halo_recv.at[1],
            right,
        ),
    ]
    spill = [
        remote(
            (own_tiles if c else tiles).at[pl.ds(BOUNDS[c], BOUNDS[c + 1] - BOUNDS[c])],
            got_tiles.at[pl.ds(BOUNDS[c], BOUNDS[c + 1] - BOUNDS[c])],
            spill_send.at[c],
            spill_recv.at[c],
            left,
        )
        for c in range(TILE_CHUNKS)
    ]
    def round_blocks(first, blocks):
        for b in range(first, first + blocks):
            ext[REACH + b] = tr[:, b * BLK : (b + 1) * BLK].astype(BF16)

    relayed = pl.ds(SPILL - RELAYED, RELAYED)
    hops = [
        remote(tiles.at[relayed], passing.at[0], hop_send.at[0], hop_recv.at[0], third),
        remote(passing.at[0], passing.at[1], hop_send.at[1], hop_recv.at[1], third),
        remote(passing.at[1], got_tiles.at[relayed], hop_send.at[2], hop_recv.at[2], last_to),
    ]
    hops[0].start()
    for copy in spill[0:1]:
        copy.start()
    load.wait()
    round_blocks(0, REACH)
    halo[0].start()
    round_blocks(REACH, BPD - REACH)
    halo[1].start()
    for copy in index_copies:
        copy.start()

    for copy in small:
        copy.wait()
    w_limit[...] = weights3(uptake_v[...].T)
    w_food[...] = weights3(preference_v[...])
    w_graze[...] = weights3(preference_v[...].T)
    w_use[...] = weights3(uptake_v[...])
    half = column_of(half_v[...])
    growth_column = column_of(growth_v[...])
    maximum = column_of(maximum_v[...])

    column_row = iota((BPD, COLS), 1)
    pick_row = (column_row >> 2) == iota((BPD, COLS), 0)
    in_block = ((iota((COLS, BLK), 0) & 3) == (iota((COLS, BLK), 1) >> 5)).astype(BF16)
    level_row = jnp.where(pick_row, levels_v[...].astype(F32), 0.0).astype(BF16)
    wet_levels = matmul(level_row, in_block)
    depth = (iota((BPD, BLK), 1) & (LEV - 1)).astype(F32)
    wet_mask = (depth < wet_levels).astype(F32)
    wet[...] = wet_mask

    def sum_plankton(i, carry):
        lanes = pl.ds(pl.multiple_of(i * BLK, BLK), BLK)
        chl[pl.ds(i, 1), :] = jnp.sum(tr[NUT : NUT + PLK, lanes], axis=0, keepdims=True)
        return carry

    lax.fori_loop(0, BPD, sum_plankton, 0, unroll=4)
    upper_row, upper_col = iota((2 * BLK, BLK), 0) & (BLK - 1), iota((2 * BLK, BLK), 1)
    above = ((upper_row < upper_col) & ((upper_row >> 5) == (upper_col >> 5))).astype(BF16)
    chl_high, chl_low = split2(chl[...] * (1.0 / PLK) * wet_mask)
    shading = matmul(jnp.concatenate([chl_high, chl_low], axis=1), above)
    sun[...] = jnp.exp(-WATER_DECAY * depth - SHADE_DECAY * shading)

    fold_col = iota((NUT, 2 * PLK), 1) & (PLK - 1)
    fold = ((fold_col >> 2) == iota((NUT, 2 * PLK), 0)).astype(BF16)
    per_group = GROUP // BLK

    def row_of(ref, i):
        return jnp.concatenate([ref[pl.ds(i * per_group + h, 1), :] for h in range(per_group)], axis=1)

    def ecosystem(i, carry):
        lanes = pl.ds(pl.multiple_of(i * GROUP, GROUP), GROUP)
        mask = row_of(wet, i) * TIMESTEP
        light = row_of(sun, i)
        nutrient = tr[:NUT, lanes]
        plankton = tr[NUT : NUT + PLK, lanes]
        detritus = tr[NUT + PLK :, lanes]
        monod = nutrient / (nutrient + half)
        limitation = matmul(w_limit[...], data3(monod))
        capacity = growth_column * (light * plankton)
        growth = capacity * limitation
        food = matmul(w_food[...], data3(plankton))
        rate = maximum * plankton / (1.0 + food)
        eaten = rate * food
        grazed = plankton * matmul(w_graze[...], data3(rate))
        mortality = MORTALITY * plankton
        d_plankton = growth - grazed + EFFICIENCY * eaten - mortality
        use = matmul(w_use[...], data3(capacity))
        d_nutrient = REMINERAL * detritus - monod * use
        waste = (1.0 - EFFICIENCY) * eaten + mortality
        d_detritus = matmul(fold, jnp.concatenate(split2(waste), axis=0)) - REMINERAL * detritus
        updated[:NUT, lanes] = nutrient + mask * d_nutrient
        updated[NUT : NUT + PLK, lanes] = plankton + mask * d_plankton
        updated[NUT + PLK :, lanes] = detritus + mask * d_detritus
        total = jnp.sum(growth, axis=0, keepdims=True)
        for h in range(per_group):
            grown[pl.ds(i * per_group + h, 1), :] = total[:, h * BLK : (h + 1) * BLK]
        return carry

    lax.fori_loop(0, CD // GROUP, ecosystem, 0)

    summed = jnp.concatenate(split3(grown[...] * (1.0 / PLK) * wet_mask), axis=1)
    lane_row, lane_col = iota((3 * BLK, COLS), 0) & (BLK - 1), iota((3 * BLK, COLS), 1)
    gather_columns = ((lane_row >> 5) == (lane_col & 3)).astype(BF16)
    by_block = matmul(summed, gather_columns)
    column_sum = jnp.sum(jnp.where(pick_row, by_block, 0.0), axis=0, keepdims=True)
    owners = owner_v[...]
    mine = (iota((n_dev, COLS), 0) == owners).astype(F32)
    earlier = (iota((COLS, COLS), 0) < iota((COLS, COLS), 1)).astype(BF16)
    seen = matmul(mine.astype(BF16), earlier)
    rank = jnp.sum(mine * seen, axis=0, keepdims=True)
    target = rank + ((owners >> 3) * share + me_z * (ny * share)).astype(F32)
    put = (iota((COLS, COLS), 0).astype(F32) == target).astype(BF16)
    to_this_z = (owners & (NZ - 1)) == iota((NZ, COLS), 0)
    sums = jnp.concatenate(split3(jnp.where(to_this_z, column_sum, 0.0)), axis=1)
    to_z[...] = matmul_nt(sums, jnp.concatenate([put, put, put], axis=1)).reshape(NZ, 1, COLS)
    from_z[me_z] = to_z[me_z]
    z_copies = [
        remote(to_z.at[lax.rem(me_z + k, NZ)], from_z.at[me_z], z_send.at[k], z_recv.at[k], z_peers[k - 1])
        for k in range(1, NZ)
    ]
    for copy in z_copies:
        copy.start()

    load_tiles.wait()
    hops[0].wait()
    hops[1].start()
    for copy in spill[1:2]:
        copy.start()
    first_row = position * BPD

    def find(rows, limit, length, steps, wanted):
        found = jnp.int32(0)
        for step in steps:
            trial = found + step
            at = rows[jnp.minimum(trial, length) - 1]
            found = jnp.where((trial <= length) & (at <= wanted), trial, found)
        last = jnp.maximum(found - 1, 0)
        return last, jnp.where((found > 0) & (rows[last] == wanted), 1, 0)

    def find_own(r, carry):
        last, held = find(tile_rows, NT, NT, (128, 64, 32, 16, 8, 4, 2, 1), first_row + r)
        place[0, r] = last
        place[1, r] = held
        return carry

    lax.fori_loop(0, BPD, find_own, 0)
    for copy in index_copies:
        copy.wait()

    def find_got(r, carry):
        last, held = find(got_rows, SPILL, SPILL, (16, 8, 4, 2, 1), first_row + r)
        got_place[0, r] = last
        got_place[1, r] = held
        return carry

    lax.fori_loop(0, BPD, find_got, 0)

    halo[0].wait_send()

    halo[0].wait_recv()
    halo[1].wait()

    first_col = first_row - REACH

    def own(t, run):
        block = jnp.clip(tile_cols[t] - first_col, 0, BPD + 2 * REACH - 1)
        term = matmul_nt(ext[block], own_tiles[t])
        goes_on = tile_rows[t] == tile_rows[jnp.maximum(t - 1, 0)]
        run = jnp.where(goes_on, run, 0.0) + term
        runs[t] = run
        return run

    run = lax.fori_loop(0, 80, own, jnp.zeros((NTR, BLK), F32), unroll=UNROLL)

    for copy in z_copies:
        copy.wait()
    over_z = from_z[0]
    for k in range(1, NZ):
        over_z += from_z[k]
    to_y[...] = over_z
    from_y[me_y] = over_z
    y_copies = [
        remote(to_y, from_y.at[me_y], y_send.at[k], y_recv.at[k], y_peers[k - 1]) for k in range(1, ny)
    ]
    for copy in y_copies:
        copy.start()

    hops[1].wait()
    hops[2].start()
    for copy in spill[2:]:
        copy.start()

    lax.fori_loop(80, NT, own, run, unroll=UNROLL)

    for r in range(BPD):
        lanes = slice(r * BLK, (r + 1) * BLK)
        updated[:, lanes] += jnp.where(place[1, r] == 1, runs[place[0, r]], 0.0)

    run = jnp.zeros((NTR, BLK), F32)
    for c in range(TILE_CHUNKS + 1):
        (spill + hops[2:])[c].wait()
        for s in range(*(BOUNDS + (SPILL,))[c : c + 2]):
            block = jnp.clip(got_cols[s] - first_col, 0, BPD + 2 * REACH - 1)
            term = matmul_nt(ext[block], got_tiles[s])
            goes_on = got_rows[s] == got_rows[max(s - 1, 0)]
            run = jnp.where(goes_on, run, 0.0) + term
            got_runs[s] = run

    for r in range(BPD):
        lanes = slice(r * BLK, (r + 1) * BLK)
        updated[:, lanes] += jnp.where(got_place[1, r] == 1, got_runs[got_place[0, r]], 0.0)

    for copy in y_copies:
        copy.wait()
    rows = jnp.concatenate([from_y[k] for k in range(ny)] + [jnp.zeros((8 - ny, COLS), F32)], axis=0)
    out_row, out_lane = iota((3 * COLS, COLS), 0) & (COLS - 1), iota((3 * COLS, COLS), 1)
    source = ((out_lane // share) & (NZ - 1)) * (ny * share) + me_y * share + (out_lane & (share - 1))
    moved = matmul(jnp.concatenate(split3(rows), axis=1), (out_row == source).astype(BF16))
    from_row = iota((8, COLS), 1) // (NZ * share) == iota((8, COLS), 0)
    production[...] = jnp.sum(jnp.where(from_row, moved, 0.0), axis=0)


def write_out(updated, production, updated_out, production_out, sem):
    copies = [
        pltpu.make_async_copy(updated, updated_out, sem.at[0]),
        pltpu.make_async_copy(production, production_out, sem.at[1]),
    ]
    for copy in copies:
        copy.start()
    for copy in copies:
        copy.wait()


def per_device(
    n_grp,
    n_dev,
    tracer,
    tile_rows,
    tile_cols,
    tile_values,
    level_counts,
    column_owner,
    half_saturation,
    growth_rate,
    uptake,
    graze_preference,
    graze_maximum,
):
    ny = n_dev // NZ
    anywhere = pl.BlockSpec(memory_space=pl.ANY)
    vector = pl.BlockSpec(memory_space=pltpu.VMEM)
    dma = pltpu.SemaphoreType.DMA
    updated, production = pl.pallas_call(
        functools.partial(kernel, n_grp, n_dev),
        out_shape=(
            pltpu.VMEM((NTR, CD), F32),
            pltpu.VMEM((COLS,), F32),
        ),
        in_specs=[anywhere] * 11,
        out_specs=(vector, vector),
        scratch_shapes=[
            pltpu.VMEM((NTR, CD), F32),
            pltpu.VMEM((BPD + 2 * REACH, NTR, BLK), BF16),
            pltpu.VMEM((NT, BLK, BLK), BF16),
            pltpu.VMEM((SPILL, BLK, BLK), BF16),
            pltpu.VMEM((NT, NTR, BLK), F32),
            pltpu.VMEM((SPILL, NTR, BLK), F32),
            pltpu.VMEM((1, COLS), jnp.int32),
            pltpu.VMEM((1, COLS), jnp.int32),
            pltpu.VMEM((1, NUT), F32),
            pltpu.VMEM((1, PLK), F32),
            pltpu.VMEM((NUT, PLK), F32),
            pltpu.VMEM((PLK, PLK), F32),
            pltpu.VMEM((1, PLK), F32),
            pltpu.VMEM((BPD, BLK), F32),
            pltpu.VMEM((BPD, BLK), F32),
            pltpu.VMEM((BPD, BLK), F32),
            pltpu.VMEM((BPD, BLK), F32),
            pltpu.VMEM((PLK, 3 * NUT), BF16),
            pltpu.VMEM((PLK, 3 * PLK), BF16),
            pltpu.VMEM((PLK, 3 * PLK), BF16),
            pltpu.VMEM((NUT, 3 * PLK), BF16),
            pltpu.VMEM((NZ, 1, COLS), F32),
            pltpu.VMEM((NZ, 1, COLS), F32),
            pltpu.VMEM((1, COLS), F32),
            pltpu.VMEM((ny, 1, COLS), F32),
            pltpu.SMEM((NT,), jnp.int32),
            pltpu.SMEM((NT,), jnp.int32),
            pltpu.SMEM((NT,), jnp.int32),
            pltpu.SMEM((NT,), jnp.int32),
            pltpu.SMEM((2, BPD), jnp.int32),
            pltpu.SMEM((2, BPD), jnp.int32),
            dma,
            dma,
            dma((SMALL,)),
            dma((2,)),
            dma((2,)),
            dma((TILE_CHUNKS,)),
            dma((TILE_CHUNKS,)),
            dma((4,)),
            dma((NZ,)),
            dma((NZ,)),
            dma((ny,)),
            dma((ny,)),
            pltpu.VMEM((2, RELAYED, BLK, BLK), BF16),
            dma((3,)),
            dma((3,)),
        ],
        compiler_params=pltpu.CompilerParams(
            collective_id=0, has_side_effects=True, vmem_limit_bytes=56 * 1024 * 1024
        ),
        name="plankton_step",
    )(
        tracer,
        tile_rows,
        tile_cols,
        tile_values,
        level_counts.reshape(1, COLS),
        column_owner.reshape(1, COLS),
        half_saturation.reshape(1, NUT),
        growth_rate.reshape(1, PLK),
        uptake.T,
        graze_preference,
        graze_maximum.reshape(1, PLK),
    )
    return pl.pallas_call(
        write_out,
        out_shape=(
            jax.ShapeDtypeStruct((NTR, CD), F32),
            jax.ShapeDtypeStruct((COLS,), F32),
        ),
        in_specs=(vector, vector),
        out_specs=(anywhere, anywhere),
        scratch_shapes=[dma((2,))],
        compiler_params=pltpu.CompilerParams(vmem_limit_bytes=1024 * 1024),
        name="write_out",
    )(updated, production)


def solution(mesh):
    n_grp, n_dev = mesh.shape["grp"], mesh.shape["dev"]
    chain = P(("grp", "dev"))
    cells = P(None, ("grp", "dev"))
    return jax.shard_map(
        functools.partial(per_device, n_grp, n_dev),
        mesh=mesh,
        in_specs=(cells, chain, chain, P(("grp", "dev"), None, None), chain, chain, P(), P(), P(), P(), P()),
        out_specs=(cells, chain),
        check_vma=False,
    )
```
